128 devices in a mesh: row: 8 (over z, core), col: 16 (over y, x).
Axes of the slice: x: 4, y: 4, z: 4, core: 2. Of those that a mesh axis runs over, the one named last changes fastest.
Arguments:
- endpoints: bfloat16 [16384, 256], P(('row', 'col')), may hold values from -30 to 30
- cells: bfloat16 [65536, 256], P('col'), may hold values from -6 to 6
Outputs:
- endpoint_potential: float32 [16384], P('row')
- cell_potential: float32 [65536], P('col')
- displacement: float32 [16384, 256], P(('row', 'col'))
The draws below stay inside these ranges and needn't reach their ends.
All inputs are finite; a program needn't handle non-finite values.
Results may differ from the reference program's by a relative error of at most 0.00045.
Values may be sent and summed in bfloat16 or wider, within the bound.
No kernel may reach another device: no remote copies, remote signals or barrier semaphores. Data moves between devices by JAX's collectives and lax.ppermute only.
A program may use at most 192 MiB of HBM per device.

```python
import math
import jax
import jax.numpy as jnp
from jax import lax

D = 256
ITERS = 3
ENDPOINTS = 16384
CELLS = 65536


def draw_endpoints(key, part):
    key = jax.random.fold_in(key, 11)
    base = jnp.clip(jax.random.normal(key, (ENDPOINTS, D), jnp.float32), -6.0, 6.0)
    return base.astype(jnp.bfloat16)


def block_scale(own_key, extent, cuts, smallest, largest):
    def one(dim, parts):
        draws = jax.random.uniform(jax.random.fold_in(jax.random.fold_in(own_key, 6), dim), (parts,), jnp.float32, smallest / len(cuts), largest / len(cuts))
        return jnp.repeat(jnp.exp(draws), extent[dim] // parts).reshape((-1,) + (1,) * (len(extent) - dim - 1))

    gain = one(*cuts[0])
    for cut in cuts[1:]:
        gain = gain * one(*cut)
    return gain


def noise(stream_key, shape, deviation, most, pieces=(), dtype=jnp.bfloat16):
    drawn = jax.random.normal(stream_key, shape, jnp.float32) * deviation
    if len(pieces) > 0:
        drawn = block_scale(stream_key, shape, pieces, -0.22, 0.18) * drawn
    return jnp.clip(drawn, min=-most, max=most).astype(dtype)


def setup_inputs(seed: int = 0) -> dict:
    splits = jax.random.split(jax.random.key(seed), 3)
    endpoints = draw_endpoints(jax.random.fold_in(splits[2], 71), 0)
    cells = noise(splits[1], (CELLS, D), 1.0, 6.0, ((0, 16),))
    return {"endpoints": endpoints, "cells": cells}


EPS = 0.1


def cost_of(xpart, ypart):
    xf = xpart.astype(jnp.float32)
    yf = ypart.astype(jnp.float32)
    xs = jnp.sum(xf * xf, axis=1)
    ys = jnp.sum(yf * yf, axis=1)
    inner = jnp.dot(xpart, ypart.T, preferred_element_type=jnp.float32)
    return (xs[:, None] + ys[None, :] - 2.0 * inner) / D


def reference(endpoints, cells):
    block_rows = math.gcd(ENDPOINTS, 1024)
    block_cols = math.gcd(CELLS, 1024)
    xblocks = endpoints.reshape(ENDPOINTS // block_rows, block_rows, D)
    yblocks = cells.reshape(CELLS // block_cols, block_cols, D)
    log_cells = jnp.float32(math.log(CELLS))
    log_ends = jnp.float32(math.log(ENDPOINTS))
    cell_pot = jnp.zeros((CELLS,), jnp.float32)
    end_pot = jnp.zeros((ENDPOINTS,), jnp.float32)
    for step in range(ITERS):
        def row_pass(xb):
            scores = (cell_pot[None, :] - cost_of(xb, cells)) / EPS
            top = jnp.max(scores, axis=1)
            lse = top + jnp.log(jnp.sum(jnp.exp(scores - top[:, None]), axis=1))
            return -EPS * (lse - log_cells)
        end_pot = lax.map(row_pass, xblocks).reshape(ENDPOINTS)

        def col_pass(yb):
            scores = (end_pot[:, None] - cost_of(endpoints, yb)) / EPS
            top = jnp.max(scores, axis=0)
            lse = top + jnp.log(jnp.sum(jnp.exp(scores - top[None, :]), axis=0))
            return -EPS * (lse - log_ends)
        cell_pot = lax.map(col_pass, yblocks).reshape(CELLS)

    fblocks = end_pot.reshape(ENDPOINTS // block_rows, block_rows)

    def grad_pass(args):
        xb, fb = args
        weight = jnp.exp((fb[:, None] + cell_pot[None, :] - cost_of(xb, cells)) / EPS - log_cells)
        mass = jnp.sum(weight, axis=1)
        moved = jnp.dot(weight.astype(jnp.bfloat16), cells, preferred_element_type=jnp.float32)
        return xb.astype(jnp.float32) * mass[:, None] - moved
    displacement = lax.map(grad_pass, (xblocks, fblocks)).reshape(ENDPOINTS, D)
    return end_pot, cell_pot, displacement
```

```python
import functools
import math

import jax
import jax.numpy as jnp
from jax import lax
from jax.experimental import pallas as pl
from jax.experimental.pallas import tpu as pltpu
from jax.sharding import PartitionSpec as P

ITERS = 3
EPS = 0.1
LOG2E = math.log2(math.e)
LIMIT = 52.0
SHIFT = 50.0
LANES = 128
TILE = 512
F32 = jnp.float32
BF16 = jnp.bfloat16
NT = (((1,), (1,)), ((), ()))


def log2(x):
    return jnp.log(x) * LOG2E


def combine(parts):
    top = jnp.max(parts, axis=0)
    return top + log2(jnp.sum(jnp.exp2(parts - top[None]), axis=0))


def fast_of(bound_ref):
    return jnp.max(bound_ref[0:1, :]) <= LIMIT


def norms(src_ref, out_ref):
    rows, depth = src_ref.shape
    step = min(TILE, rows)
    ones = jnp.ones((8, depth), BF16)
    for t in range(rows // step):
        val = src_ref[t * step : (t + 1) * step, :].astype(F32)
        sq = val * val
        high = sq.astype(BF16)
        low = (sq - high.astype(F32)).astype(BF16)
        got = lax.dot_general(ones, high, NT, preferred_element_type=F32)
        got = got + lax.dot_general(ones, low, NT, preferred_element_type=F32)
        for k in range(step // LANES):
            row = t * (step // LANES) + k
            out_ref[row : row + 1, :] = got[0:1, k * LANES : (k + 1) * LANES]


def spread(rows, out_ref):
    for b in range(rows.shape[0]):
        out_ref[b * LANES : (b + 1) * LANES, :] = jnp.broadcast_to(rows[b : b + 1, :], (LANES, LANES)).T


def gather_rows(src_ref, out_ref):
    for b in range(src_ref.shape[0] // LANES):
        block = src_ref[b * LANES : (b + 1) * LANES, :].T
        out_ref[b : b + 1, :] = jnp.sum(block, axis=0, keepdims=True)


def first_rows(src_ref, out_ref):
    for b in range(src_ref.shape[0] // LANES):
        block = src_ref[b * LANES : (b + 1) * LANES, :].T
        out_ref[b : b + 1, :] = block[0:1, :]


def careful_rows(m_ref, c_ref, acc_ref, top_ref):
    slabs, rows, _ = m_ref.shape
    step = 64

    def body(r, carry):
        here = pl.ds(pl.multiple_of(r * step, step), step)

        def score(s, k):
            row = s * (TILE // LANES) + k
            return m_ref[s, here, k * LANES : (k + 1) * LANES] + c_ref[row : row + 1, :]

        each = [(s, k) for s in range(slabs) for k in range(TILE // LANES)]
        top = functools.reduce(jnp.maximum, [score(s, k) for s, k in each])
        top = jnp.broadcast_to(jnp.max(top, axis=1, keepdims=True), top.shape)
        acc_ref[here, :] = functools.reduce(jnp.add, [jnp.exp2(score(s, k) - top) for s, k in each])
        top_ref[here, :] = top
        return carry

    lax.fori_loop(0, rows // step, body, 0)


def fast_rows(m_ref, v_ref, acc_ref):
    slabs, rows, _ = m_ref.shape
    step = 64

    def body(r, carry):
        here = pl.ds(pl.multiple_of(r * step, step), step)
        total = None
        for s in range(slabs):
            for k in range(TILE // LANES):
                row = s * (TILE // LANES) + k
                term = m_ref[s, here, k * LANES : (k + 1) * LANES] * v_ref[row : row + 1, :]
                total = term if total is None else total + term
        acc_ref[here, :] = total
        return carry

    lax.fori_loop(0, rows // step, body, 0)


def finish_rows(fast, shift, acc_ref, top_ref, bits_ref, row_ref, out_ref):
    gather_rows(acc_ref, row_ref)

    @pl.when(fast)
    def _():
        bits_ref[...] = jnp.broadcast_to(shift, bits_ref.shape)

    @pl.when(jnp.logical_not(fast))
    def _():
        first_rows(top_ref, bits_ref)

    out_ref[...] = jnp.broadcast_to((log2(row_ref[...]) + bits_ref[...])[None], out_ref.shape)


def first_kernel(x_ref, y_ref, m_ref, bound_ref, ynorm_ref, xnorm_ref, out_ref, v_ref, acc_ref, top_ref, bits_ref, row_ref):
    rows, depth = x_ref.shape
    slabs = m_ref.shape[0]
    scale = 2.0 * LOG2E / (EPS * depth)
    norms(y_ref, ynorm_ref)
    norms(x_ref, xnorm_ref)
    most_x = jnp.max(xnorm_ref[...], keepdims=True)
    most_y = jnp.max(ynorm_ref[...], keepdims=True)
    bound = scale * jnp.sqrt(most_x * most_y)
    bound_ref[...] = jnp.broadcast_to(bound, bound_ref.shape)
    fast = jnp.max(bound) <= LIMIT
    c_bits = ynorm_ref[...] * (-LOG2E / (EPS * depth))
    top_c = jnp.max(c_bits, keepdims=True)

    step = min(512, rows)

    def scores(s, here):
        ys = y_ref[pl.ds(pl.multiple_of(s * TILE, TILE), TILE), :]
        return lax.dot_general(x_ref[here, :], ys, NT, preferred_element_type=F32) * scale

    @pl.when(fast)
    def _():
        v_ref[...] = jnp.exp2(c_bits - top_c + SHIFT)
        acc_ref[...] = jnp.zeros_like(acc_ref)

        def slab(s, carry):
            def body(r, carry):
                here = pl.ds(pl.multiple_of(r * step, step), step)
                power = jnp.exp2(scores(s, here))
                m_ref[s, here, :] = power
                total = acc_ref[here, :]
                for k in range(TILE // LANES):
                    total = total + power[:, k * LANES : (k + 1) * LANES] * v_ref[pl.ds(s * (TILE // LANES) + k, 1), :]
                acc_ref[here, :] = total
                return carry

            return lax.fori_loop(0, rows // step, body, carry)

        lax.fori_loop(0, slabs, slab, 0)

    @pl.when(jnp.logical_not(fast))
    def _():
        v_ref[...] = c_bits

        def slab(s, carry):
            def body(r, carry):
                here = pl.ds(pl.multiple_of(r * step, step), step)
                m_ref[s, here, :] = scores(s, here)
                return carry

            return lax.fori_loop(0, rows // step, body, carry)

        lax.fori_loop(0, slabs, slab, 0)
        careful_rows(m_ref, v_ref, acc_ref, top_ref)

    finish_rows(fast, top_c - SHIFT, acc_ref, top_ref, bits_ref, row_ref, out_ref)


def row_kernel(log_ends, m_ref, bound_ref, got_ref, out_ref, v_ref, acc_ref, top_ref, bits_ref, row_ref):
    fast = fast_of(bound_ref)
    c_bits = log_ends - combine(got_ref[...])
    top_c = jnp.max(c_bits, keepdims=True)

    @pl.when(fast)
    def _():
        v_ref[...] = jnp.exp2(c_bits - top_c + SHIFT)
        fast_rows(m_ref, v_ref, acc_ref)

    @pl.when(jnp.logical_not(fast))
    def _():
        v_ref[...] = c_bits
        careful_rows(m_ref, v_ref, acc_ref, top_ref)

    finish_rows(fast, top_c - SHIFT, acc_ref, top_ref, bits_ref, row_ref, out_ref)


def col_kernel(log_cells, m_ref, bound_ref, got_ref, out_ref, u_ref, sum_ref):
    slabs, rows, _ = m_ref.shape
    fast = fast_of(bound_ref)
    f_bits = log_cells - combine(got_ref[...])
    top_f = jnp.max(f_bits, keepdims=True)
    step = 64

    @pl.when(fast)
    def _():
        spread(jnp.exp2(f_bits - top_f + SHIFT), u_ref)
        wide = 2 if slabs % 2 == 0 else 1
        for s in range(0, slabs, wide):

            def body(r, totals):
                here = pl.ds(pl.multiple_of(r * step, step), step)
                u = u_ref[here, :]
                new = []
                for w in range(wide):
                    for k in range(TILE // LANES):
                        term = m_ref[s + w, here, k * LANES : (k + 1) * LANES] * u
                        total = totals[len(new)]
                        for g in range(step // 8):
                            total = total + term[g * 8 : (g + 1) * 8, :]
                        new.append(total)
                return tuple(new)

            n = wide * (TILE // LANES)
            totals = lax.fori_loop(0, rows // step, body, (jnp.zeros((8, LANES), F32),) * n)
            for k in range(n):
                row = s * (TILE // LANES) + k
                sum_ref[row : row + 1, :] = jnp.sum(totals[k], axis=0, keepdims=True)
        sum_ref[...] = log2(sum_ref[...]) + (top_f - SHIFT)

    @pl.when(jnp.logical_not(fast))
    def _():
        spread(f_bits, u_ref)
        for s in range(slabs):
            for k in range(TILE // LANES):

                def score(r):
                    here = pl.ds(pl.multiple_of(r * step, step), step)
                    return m_ref[s, here, k * LANES : (k + 1) * LANES] + u_ref[here, :]

                def most(r, top):
                    return jnp.maximum(top, score(r))

                top = lax.fori_loop(0, rows // step, most, jnp.full((step, LANES), -3.0e38, F32))
                top = jnp.max(top, axis=0, keepdims=True)

                def add(r, total):
                    return total + jnp.exp2(score(r) - top)

                total = lax.fori_loop(0, rows // step, add, jnp.zeros((step, LANES), F32))
                row = s * (TILE // LANES) + k
                sum_ref[row : row + 1, :] = log2(jnp.sum(total, axis=0, keepdims=True)) + top

    out_ref[...] = jnp.broadcast_to(sum_ref[...][None], out_ref.shape)


def last_kernel(log_cells, log_ends, m_ref, bound_ref, rows_ref, cols_ref, y_ref, xnorm_ref, ynorm_ref,
                end_ref, cell_ref, out_ref, u_ref, v_ref, mass_ref, row_ref):
    slabs, rows, _ = m_ref.shape
    depth = y_ref.shape[1]
    fast = fast_of(bound_ref)
    f_bits = log_cells - combine(rows_ref[...])
    c_bits = log_ends - combine(cols_ref[...])
    end_ref[...] = f_bits * (EPS / LOG2E) + xnorm_ref[...] * (1.0 / depth)
    cell_ref[...] = c_bits * (EPS / LOG2E) + ynorm_ref[...] * (1.0 / depth)
    top_f = jnp.max(f_bits, keepdims=True) - 24.0
    step = min(256, rows)

    def weigh(weight):
        def body(r, carry):
            here = pl.ds(pl.multiple_of(r * step, step), step)
            u = u_ref[here, :]
            moved = None
            mass = None
            for s in range(slabs):
                parts = []
                for k in range(TILE // LANES):
                    row = s * (TILE // LANES) + k
                    part = weight(m_ref[s, here, k * LANES : (k + 1) * LANES], u, v_ref[row : row + 1, :])
                    mass = part if mass is None else mass + part
                    parts.append(part.astype(BF16))
                term = jnp.dot(
                    jnp.concatenate(parts, axis=1), y_ref[s * TILE : (s + 1) * TILE, :], preferred_element_type=F32
                )
                moved = term if moved is None else moved + term
            mass_ref[here, :] = mass
            for g in range(step // LANES):
                out_ref[r * (step // LANES) + g, 0:LANES, :] = moved[g * LANES : (g + 1) * LANES, :].astype(BF16)
            return carry

        lax.fori_loop(0, rows // step, body, 0)

    @pl.when(fast)
    def _():
        spread(jnp.exp2(f_bits - top_f), u_ref)
        v_ref[...] = jnp.exp2(c_bits + (top_f - log_cells))
        weigh(lambda m, u, v: (m * u) * v)

    @pl.when(jnp.logical_not(fast))
    def _():
        spread(f_bits, u_ref)
        v_ref[...] = c_bits - log_cells
        weigh(lambda m, u, v: jnp.exp2((m + u) + v))

    gather_rows(mass_ref, row_ref)
    for b in range(rows // LANES):
        mass = jnp.broadcast_to(row_ref[b : b + 1, :], (16, LANES))
        high = mass.astype(BF16)
        rest = mass - high.astype(F32)
        mid = rest.astype(BF16)
        low = (rest - mid.astype(F32)).astype(BF16)
        out_ref[b, LANES : LANES + 16, :] = jnp.concatenate([high, mid], axis=1)
        out_ref[b, LANES + 16 : LANES + 32, :] = jnp.concatenate([low, low], axis=1)


def end_kernel(got_ref, x_ref, out_ref):
    moved = got_ref[0, 0:LANES, :].astype(F32)
    high = got_ref[0, LANES : LANES + 16, :].astype(F32)
    low = got_ref[0, LANES + 16 : LANES + 32, :].astype(F32)
    mass = (high[:, :LANES] + high[:, LANES:]) + low[:, :LANES]
    for n in range(1, got_ref.shape[0]):
        moved = moved + got_ref[n, 0:LANES, :].astype(F32)
        high = got_ref[n, LANES : LANES + 16, :].astype(F32)
        low = got_ref[n, LANES + 16 : LANES + 32, :].astype(F32)
        mass = mass + ((high[:, :LANES] + high[:, LANES:]) + low[:, :LANES])
    wide = jnp.broadcast_to(mass[0:1, :], (LANES, LANES)).T
    x = x_ref[...].astype(F32)
    out_ref[:, :LANES] = x[:, :LANES] * wide - moved[:, :LANES]
    out_ref[:, LANES:] = x[:, LANES:] * wide - moved[:, LANES:]


def call(kernel, outs, scratch, limit_mib=26):
    return pl.pallas_call(
        kernel,
        out_shape=outs,
        scratch_shapes=[pltpu.VMEM(s, F32) for s in scratch],
        compiler_params=pltpu.CompilerParams(vmem_limit_bytes=limit_mib << 20),
    )


def swap(parts, axis):
    return lax.all_to_all(parts, axis, 0, 0, tiled=True)


def pin(m):
    return pltpu.with_memory_space_constraint(m, pltpu.VMEM)


def shards(endpoints, cells):
    n_row, n_col = lax.axis_size("row"), lax.axis_size("col")
    own, depth = endpoints.shape
    rows, cols = own * n_col, cells.shape[0]
    log_cells = math.log2(cols * n_col)
    log_ends = math.log2(rows * n_row)
    rb, cb = rows // LANES, cols // LANES
    block_x = swap(jnp.broadcast_to(endpoints[None], (n_col, own, depth)), "col").reshape(rows, depth)

    arr = lambda *shape: jax.ShapeDtypeStruct(shape, F32)
    row_scratch = [(cb, LANES), (rows, LANES), (rows, LANES), (rb, LANES), (rb, LANES)]
    col_scratch = [(rows, LANES), (cb, LANES)]
    m, bound, ynorm, xnorm, sums = call(
        first_kernel,
        [pltpu.VMEM((cols // TILE, rows, TILE), F32), arr(8, LANES), arr(cb, LANES), arr(rb, LANES), arr(n_col, rb, LANES)],
        row_scratch,
    )(block_x, cells)
    for step in range(ITERS):
        if step > 0:
            sums = call(functools.partial(row_kernel, log_ends), arr(n_col, rb, LANES), row_scratch)(pin(m), bound, got_cols)
        got_rows = swap(sums, "col")
        sums = call(functools.partial(col_kernel, log_cells), arr(n_row, cb, LANES), col_scratch)(pin(m), bound, got_rows)
        got_cols = swap(sums, "row")
    end_pot, cell_pot, moved = call(
        functools.partial(last_kernel, log_cells, log_ends),
        [arr(rb, LANES), arr(cb, LANES), jax.ShapeDtypeStruct((n_col, own + 32, depth), BF16)],
        [(rows, LANES), (cb, LANES), (rows, LANES), (rb, LANES)],
    )(pin(m), bound, got_rows, got_cols, cells, xnorm, ynorm)
    displacement = call(end_kernel, arr(own, depth), [])(swap(moved, "col"), endpoints)
    return end_pot.reshape(rows), cell_pot.reshape(cols), displacement


def solution(mesh):
    return jax.shard_map(
        shards,
        mesh=mesh,
        in_specs=(P(("row", "col"), None), P("col", None)),
        out_specs=(P("row"), P("col"), P(("row", "col"), None)),
        check_vma=False,
    )
```

```python
import functools
import math

import jax
import jax.numpy as jnp
from jax import lax
from jax.experimental import pallas as pl
from jax.experimental.pallas import tpu as pltpu
from jax.sharding import PartitionSpec as P

ITERS = 3
EPS = 0.1
LOG2E = math.log2(math.e)
LIMIT = 52.0
SHIFT = 50.0
LANES = 128
TILE = 512
F32 = jnp.float32
BF16 = jnp.bfloat16
NT = (((1,), (1,)), ((), ()))


def log2(x):
    return jnp.log(x) * LOG2E


def combine(parts):
    top = jnp.max(parts, axis=0)
    return top + log2(jnp.sum(jnp.exp2(parts - top[None]), axis=0))


def fast_of(bound_ref):
    return jnp.max(bound_ref[0:1, :]) <= LIMIT


def norms(src_ref, out_ref):
    rows, depth = src_ref.shape
    step = min(TILE, rows)
    ones = jnp.ones((8, depth), BF16)
    for t in range(rows // step):
        val = src_ref[t * step : (t + 1) * step, :].astype(F32)
        sq = val * val
        high = sq.astype(BF16)
        low = (sq - high.astype(F32)).astype(BF16)
        got = lax.dot_general(ones, high, NT, preferred_element_type=F32)
        got = got + lax.dot_general(ones, low, NT, preferred_element_type=F32)
        for k in range(step // LANES):
            row = t * (step // LANES) + k
            out_ref[row : row + 1, :] = got[0:1, k * LANES : (k + 1) * LANES]


def spread(rows, out_ref):
    for b in range(rows.shape[0]):
        out_ref[b * LANES : (b + 1) * LANES, :] = jnp.broadcast_to(rows[b : b + 1, :], (LANES, LANES)).T


def gather_rows(src_ref, out_ref):
    for b in range(src_ref.shape[0] // LANES):
        block = src_ref[b * LANES : (b + 1) * LANES, :].T
        out_ref[b : b + 1, :] = jnp.sum(block, axis=0, keepdims=True)


def first_rows(src_ref, out_ref):
    for b in range(src_ref.shape[0] // LANES):
        block = src_ref[b * LANES : (b + 1) * LANES, :].T
        out_ref[b : b + 1, :] = block[0:1, :]


def careful_rows(m_ref, c_ref, acc_ref, top_ref):
    slabs, rows = len(m_ref), m_ref[0].shape[0]
    step = 64

    def body(r, carry):
        here = pl.ds(pl.multiple_of(r * step, step), step)

        def score(s, k):
            row = s * (TILE // LANES) + k
            return m_ref[s][here, k * LANES : (k + 1) * LANES] + c_ref[row : row + 1, :]

        each = [(s, k) for s in range(slabs) for k in range(TILE // LANES)]
        top = functools.reduce(jnp.maximum, [score(s, k) for s, k in each])
        top = jnp.broadcast_to(jnp.max(top, axis=1, keepdims=True), top.shape)
        acc_ref[here, :] = functools.reduce(jnp.add, [jnp.exp2(score(s, k) - top) for s, k in each])
        top_ref[here, :] = top
        return carry

    lax.fori_loop(0, rows // step, body, 0)


def fast_rows(m_ref, v_ref, acc_ref):
    slabs, rows = len(m_ref), m_ref[0].shape[0]
    step = 256

    def body(r, carry):
        here = pl.ds(pl.multiple_of(r * step, step), step)
        total = None
        for s in range(slabs):
            for k in range(TILE // LANES):
                row = s * (TILE // LANES) + k
                term = m_ref[s][here, k * LANES : (k + 1) * LANES] * v_ref[row : row + 1, :]
                total = term if total is None else total + term
        acc_ref[here, :] = total
        return carry

    lax.fori_loop(0, rows // step, body, 0, unroll=2)


def finish_rows(fast, shift, acc_ref, top_ref, bits_ref, row_ref, out_ref):
    gather_rows(acc_ref, row_ref)

    @pl.when(fast)
    def _():
        bits_ref[...] = jnp.broadcast_to(shift, bits_ref.shape)

    @pl.when(jnp.logical_not(fast))
    def _():
        first_rows(top_ref, bits_ref)

    out_ref[...] = jnp.broadcast_to((log2(row_ref[...]) + bits_ref[...])[None], out_ref.shape)


def cells_kernel(y_ref, ynorm_ref):
    norms(y_ref, ynorm_ref)


def first_kernel(x_ref, y_ref, ynorm_ref, m_ref, bound_ref, xnorm_ref, out_ref, v_ref, acc_ref, top_ref, bits_ref, row_ref):
    rows, depth = x_ref.shape
    slabs = len(m_ref)
    scale = 2.0 * LOG2E / (EPS * depth)
    norms(x_ref, xnorm_ref)
    most_x = jnp.max(xnorm_ref[...], keepdims=True)
    most_y = jnp.max(ynorm_ref[...], keepdims=True)
    bound = scale * jnp.sqrt(most_x * most_y)
    bound_ref[...] = jnp.broadcast_to(bound, bound_ref.shape)
    fast = jnp.max(bound) <= LIMIT
    c_bits = ynorm_ref[...] * (-LOG2E / (EPS * depth))
    top_c = jnp.max(c_bits, keepdims=True)

    step = min(512, rows)

    def scores(s, here):
        ys = y_ref[s * TILE : (s + 1) * TILE, :]
        return lax.dot_general(x_ref[here, :], ys, NT, preferred_element_type=F32) * scale

    @pl.when(fast)
    def _():
        v_ref[...] = jnp.exp2(c_bits - top_c + SHIFT)
        for s in range(slabs):
            for r in range(rows // step):
                here = slice(r * step, (r + 1) * step)
                power = jnp.exp2(scores(s, here))
                m_ref[s][here, :] = power
                total = None if s == 0 else acc_ref[here, :]
                for k in range(TILE // LANES):
                    row = s * (TILE // LANES) + k
                    term = power[:, k * LANES : (k + 1) * LANES] * v_ref[row : row + 1, :]
                    total = term if total is None else total + term
                acc_ref[here, :] = total

    @pl.when(jnp.logical_not(fast))
    def _():
        v_ref[...] = c_bits

        for s in range(slabs):
            m_ref[s][...] = scores(s, slice(None))
        careful_rows(m_ref, v_ref, acc_ref, top_ref)

    finish_rows(fast, top_c - SHIFT, acc_ref, top_ref, bits_ref, row_ref, out_ref)


def row_kernel(log_ends, m_ref, bound_ref, got_ref, out_ref, v_ref, acc_ref, top_ref, bits_ref, row_ref):
    fast = fast_of(bound_ref)
    c_bits = log_ends - combine(got_ref[...])
    top_c = jnp.max(c_bits, keepdims=True)

    @pl.when(fast)
    def _():
        v_ref[...] = jnp.exp2(c_bits - top_c + SHIFT)
        fast_rows(m_ref, v_ref, acc_ref)

    @pl.when(jnp.logical_not(fast))
    def _():
        v_ref[...] = c_bits
        careful_rows(m_ref, v_ref, acc_ref, top_ref)

    finish_rows(fast, top_c - SHIFT, acc_ref, top_ref, bits_ref, row_ref, out_ref)


def col_kernel(log_cells, m_ref, bound_ref, got_ref, out_ref, u_ref, sum_ref):
    slabs, rows = len(m_ref), m_ref[0].shape[0]
    fast = fast_of(bound_ref)
    f_bits = log_cells - combine(got_ref[...])
    top_f = jnp.max(f_bits, keepdims=True)
    step = 64

    @pl.when(fast)
    def _():
        spread(jnp.exp2(f_bits - top_f + SHIFT), u_ref)
        wide = 8 if slabs % 8 == 0 else 1
        for s in range(0, slabs, wide):

            def body(r, totals):
                here = pl.ds(pl.multiple_of(r * step, step), step)
                u = u_ref[here, :]
                new = []
                for w in range(wide):
                    for k in range(TILE // LANES):
                        term = m_ref[s + w][here, k * LANES : (k + 1) * LANES] * u
                        total = totals[len(new)]
                        for g in range(step // 8):
                            total = total + term[g * 8 : (g + 1) * 8, :]
                        new.append(total)
                return tuple(new)

            n = wide * (TILE // LANES)
            totals = lax.fori_loop(0, rows // step, body, (jnp.zeros((8, LANES), F32),) * n, unroll=2)
            for k in range(n):
                row = s * (TILE // LANES) + k
                sum_ref[row : row + 1, :] = jnp.sum(totals[k], axis=0, keepdims=True)
        sum_ref[...] = log2(sum_ref[...]) + (top_f - SHIFT)

    @pl.when(jnp.logical_not(fast))
    def _():
        spread(f_bits, u_ref)
        for s in range(slabs):
            for k in range(TILE // LANES):

                def score(r):
                    here = pl.ds(pl.multiple_of(r * step, step), step)
                    return m_ref[s][here, k * LANES : (k + 1) * LANES] + u_ref[here, :]

                def most(r, top):
                    return jnp.maximum(top, score(r))

                top = lax.fori_loop(0, rows // step, most, jnp.full((step, LANES), -3.0e38, F32))
                top = jnp.max(top, axis=0, keepdims=True)

                def add(r, total):
                    return total + jnp.exp2(score(r) - top)

                total = lax.fori_loop(0, rows // step, add, jnp.zeros((step, LANES), F32))
                row = s * (TILE // LANES) + k
                sum_ref[row : row + 1, :] = log2(jnp.sum(total, axis=0, keepdims=True)) + top

    out_ref[...] = jnp.broadcast_to(sum_ref[...][None], out_ref.shape)


def last_kernel(log_cells, log_ends, m_ref, bound_ref, rows_ref, cols_ref, y_ref, xnorm_ref, ynorm_ref,
                end_ref, cell_ref, out_ref, u_ref, v_ref, mass_ref, row_ref):
    slabs, rows = len(m_ref), m_ref[0].shape[0]
    depth = y_ref.shape[1]
    fast = fast_of(bound_ref)
    f_bits = log_cells - combine(rows_ref[...])
    c_bits = log_ends - combine(cols_ref[...])
    end_ref[...] = f_bits * (EPS / LOG2E) + xnorm_ref[...] * (1.0 / depth)
    cell_ref[...] = c_bits * (EPS / LOG2E) + ynorm_ref[...] * (1.0 / depth)
    top_f = jnp.max(f_bits, keepdims=True) - 24.0
    step = min(1024, rows)

    def weigh(weight):
        def body(r, carry):
            here = pl.ds(pl.multiple_of(r * step, step), step)
            u = u_ref[here, :]
            moved = None
            mass = None
            for s in range(slabs):
                parts = []
                for k in range(TILE // LANES):
                    row = s * (TILE // LANES) + k
                    part = weight(m_ref[s][here, k * LANES : (k + 1) * LANES], u, v_ref[row : row + 1, :])
                    mass = part if mass is None else mass + part
                    parts.append(part.astype(BF16))
                term = jnp.dot(
                    jnp.concatenate(parts, axis=1), y_ref[s * TILE : (s + 1) * TILE, :], preferred_element_type=F32
                )
                moved = term if moved is None else moved + term
            mass_ref[here, :] = mass
            for g in range(step // LANES):
                out_ref[r * (step // LANES) + g, 0:LANES, :] = moved[g * LANES : (g + 1) * LANES, :].astype(BF16)
            return carry

        lax.fori_loop(0, rows // step, body, 0)

    @pl.when(fast)
    def _():
        spread(jnp.exp2(f_bits - top_f), u_ref)
        v_ref[...] = jnp.exp2(c_bits + (top_f - log_cells))
        weigh(lambda m, u, v: (m * u) * v)

    @pl.when(jnp.logical_not(fast))
    def _():
        spread(f_bits, u_ref)
        v_ref[...] = c_bits - log_cells
        weigh(lambda m, u, v: jnp.exp2((m + u) + v))

    gather_rows(mass_ref, row_ref)
    for b in range(rows // LANES):
        mass = jnp.broadcast_to(row_ref[b : b + 1, :], (8, LANES))
        high = mass.astype(BF16).astype(F32)
        mid = (mass - high).astype(BF16).astype(F32)
        low = mass - high - mid
        first = jnp.concatenate([high, mid], axis=1)
        second = jnp.concatenate([low, low], axis=1)
        out_ref[b, LANES : LANES + 16, :] = jnp.concatenate([first, second], axis=0).astype(BF16)


def end_kernel(got_ref, x_ref, out_ref):
    moved, mass = None, None
    for n in range(got_ref.shape[0]):
        part = got_ref[n, 0:LANES, :].astype(F32)
        parts = got_ref[n, LANES : LANES + 16, :].astype(F32)
        weight = (parts[0:1, :LANES] + parts[0:1, LANES:]) + parts[8:9, :LANES]
        moved = part if moved is None else moved + part
        mass = weight if mass is None else mass + weight
    wide = jnp.broadcast_to(mass, (LANES, LANES)).T
    x = x_ref[...].astype(F32)
    out_ref[:, :LANES] = x[:, :LANES] * wide - moved[:, :LANES]
    out_ref[:, LANES:] = x[:, LANES:] * wide - moved[:, LANES:]


def call(kernel, outs, scratch, limit_mib=16, cost=None):
    return pl.pallas_call(
        kernel,
        name=getattr(kernel, "func", kernel).__name__,
        out_shape=outs,
        cost_estimate=cost,
        scratch_shapes=[pltpu.VMEM(s, F32) if isinstance(s, tuple) else s for s in scratch],
        compiler_params=pltpu.CompilerParams(vmem_limit_bytes=limit_mib << 20),
    )


def swap(parts, axis):
    return lax.all_to_all(parts, axis, 0, 0, tiled=True)


def grouped(kernel, at, count):
    def body(*refs):
        kernel(*refs[:at], refs[at : at + count], *refs[at + count :])

    body.__name__ = getattr(kernel, "func", kernel).__name__
    return body


def pin(m):
    return pltpu.with_memory_space_constraint(m, pltpu.VMEM)


def shards(endpoints, cells):
    n_row, n_col = lax.axis_size("row"), lax.axis_size("col")
    own, depth = endpoints.shape
    rows, cols = own * n_col, cells.shape[0]
    log_cells = math.log2(cols * n_col)
    log_ends = math.log2(rows * n_row)
    rb, cb = rows // LANES, cols // LANES
    block_x = swap(jnp.broadcast_to(endpoints[None], (n_col, own, depth)), "col").reshape(rows, depth)

    arr = lambda *shape: pltpu.VMEM(shape, F32)
    hbm = lambda *shape: jax.ShapeDtypeStruct(shape, F32)
    row_scratch = [(cb, LANES), (rows, LANES), (rows, LANES), (rb, LANES), (rb, LANES)]
    col_scratch = [(rows, LANES), (cb, LANES)]
    cost = pl.CostEstimate(flops=cols * depth * 64, bytes_accessed=4 * cols * depth, transcendentals=0)
    ynorm = call(cells_kernel, arr(cb, LANES), [], cost=cost)(pin(cells))
    slabs = cols // TILE
    *m, bound, xnorm, sums = call(
        grouped(first_kernel, 3, slabs),
        [pltpu.VMEM((rows, TILE), F32)] * slabs + [arr(8, LANES), arr(rb, LANES), arr(n_col, rb, LANES)],
        row_scratch,
    )(pin(block_x), pin(cells), pin(ynorm))
    for step in range(ITERS):
        if step > 0:
            sums = call(grouped(functools.partial(row_kernel, log_ends), 0, slabs), arr(n_col, rb, LANES), row_scratch)(*map(pin, m), pin(bound), pin(got_cols))
        got_rows = swap(sums, "col")
        sums = call(grouped(functools.partial(col_kernel, log_cells), 0, slabs), arr(n_row, cb, LANES), col_scratch)(*map(pin, m), pin(bound), pin(got_rows))
        got_cols = swap(sums, "row")
    end_pot, cell_pot, moved = call(
        grouped(functools.partial(last_kernel, log_cells, log_ends), 0, slabs),
        [hbm(rb, LANES), hbm(cb, LANES), pltpu.VMEM((n_col, own + 16, depth), BF16)],
        [(rows, LANES), (cb, LANES), (rows, LANES), (rb, LANES)],
    )(*map(pin, m), pin(bound), pin(got_rows), pin(got_cols), pin(cells), pin(xnorm), pin(ynorm))
    displacement = call(end_kernel, hbm(own, depth), [])(pin(swap(moved, "col")), endpoints)
    return end_pot.reshape(rows), cell_pot.reshape(cols), displacement


def solution(mesh):
    return jax.shard_map(
        shards,
        mesh=mesh,
        in_specs=(P(("row", "col"), None), P("col", None)),
        out_specs=(P("row"), P("col"), P(("row", "col"), None)),
        check_vma=False,
    )
```

```python
import functools
import math

import jax
import jax.numpy as jnp
from jax import lax
from jax.experimental import pallas as pl
from jax.experimental.pallas import tpu as pltpu
from jax.sharding import PartitionSpec as P

ITERS = 3
EPS = 0.1
LOG2E = math.log2(math.e)
LIMIT = 52.0
SHIFT = 50.0
LANES = 128
TILE = 512
F32 = jnp.float32
BF16 = jnp.bfloat16
NT = (((1,), (1,)), ((), ()))


def log2(x):
    return jnp.log(x) * LOG2E


def combine(parts):
    top = jnp.max(parts, axis=0)
    return top + log2(jnp.sum(jnp.exp2(parts - top[None]), axis=0))


def norms(src_ref, out_ref):
    rows, depth = src_ref.shape
    step = min(TILE, rows)
    ones = jnp.ones((8, depth), BF16)
    for t in range(rows // step):
        val = src_ref[t * step : (t + 1) * step, :].astype(F32)
        sq = val * val
        high = sq.astype(BF16)
        low = (sq - high.astype(F32)).astype(BF16)
        got = lax.dot_general(ones, high, NT, preferred_element_type=F32)
        got = got + lax.dot_general(ones, low, NT, preferred_element_type=F32)
        for k in range(step // LANES):
            row = t * (step // LANES) + k
            out_ref[row : row + 1, :] = got[0:1, k * LANES : (k + 1) * LANES]


def holder(b, nx, ny):
    g, d = divmod(b, nx)
    turned = d * ny + g if nx == ny else b
    odd = lax.rem(lax.axis_index("row"), 2) == 1
    return lax.axis_index("col") ^ jnp.where(odd, turned, b)


def spread(row, out_ref, at):
    out_ref[at : at + LANES, :] = jnp.broadcast_to(row, (LANES, LANES)).T


def lane_sums(block):
    return jnp.sum(block.T, axis=0, keepdims=True)


def is_fast(bound_ref):
    return jnp.max(bound_ref[0:1, :]) <= LIMIT


def all_fast(bounds):
    return jnp.max(functools.reduce(jnp.maximum, [b[0:1, :] for b in bounds])) <= LIMIT


def score_of(fast, m):
    return jnp.where(fast, log2(m), m)


def careful_rows(slabs, fast, c_ref, acc_ref, top_ref, at):
    step = 64

    def body(r, carry):
        here = pl.ds(pl.multiple_of(r * step, step), step)
        there = pl.ds(pl.multiple_of(at + r * step, step), step)

        def score(s, k):
            row = s * (TILE // LANES) + k
            return score_of(fast, slabs[s][here, k * LANES : (k + 1) * LANES]) + c_ref[row : row + 1, :]

        each = [(s, k) for s in range(len(slabs)) for k in range(TILE // LANES)]
        top = functools.reduce(jnp.maximum, [score(s, k) for s, k in each])
        top = jnp.broadcast_to(jnp.max(top, axis=1, keepdims=True), top.shape)
        acc_ref[there, :] = functools.reduce(jnp.add, [jnp.exp2(score(s, k) - top) for s, k in each])
        top_ref[there, :] = top
        return carry

    lax.fori_loop(0, slabs[0].shape[0] // step, body, 0)


def fast_rows(slabs, v_ref, acc_ref, at):
    step = min(256, slabs[0].shape[0])
    for r in range(slabs[0].shape[0] // step):
        total = None
        for s in range(len(slabs)):
            for k in range(TILE // LANES):
                row = s * (TILE // LANES) + k
                term = slabs[s][r * step : (r + 1) * step, k * LANES : (k + 1) * LANES] * v_ref[row : row + 1, :]
                total = term if total is None else total + term
        acc_ref[at + r * step : at + (r + 1) * step, :] = total


def cells_kernel(y_ref, ynorm_ref):
    norms(y_ref, ynorm_ref)


def join_kernel(ynorm_ref, got_refs, out_ref, start_ref):
    for d, got_ref in enumerate(got_refs):
        out_ref[d * LANES : (d + 1) * LANES, :] = got_ref[...]
    start_ref[...] = ynorm_ref[0 : start_ref.shape[0], :]


def first_kernel(g, x_ref, y_ref, ynorm_ref, before_ref, m_ref, bound_ref, xnorm_ref, out_ref,
                 v_ref, acc_ref, top_ref, row_ref):
    rows, depth = x_ref.shape
    blocks = rows // LANES
    slabs = len(m_ref)
    scale = 2.0 * LOG2E / (EPS * depth)
    norms(x_ref, xnorm_ref)
    most_x = jnp.max(xnorm_ref[0:blocks, :], keepdims=True)
    most_y = jnp.max(ynorm_ref[...], keepdims=True)
    bound = scale * jnp.sqrt(most_x * most_y)
    bound_ref[...] = jnp.broadcast_to(bound, bound_ref.shape)
    fast = jnp.max(bound) <= LIMIT
    c_bits = ynorm_ref[...] * (-LOG2E / (EPS * depth))
    top_c = jnp.max(c_bits, keepdims=True)

    def scores(s):
        ys = y_ref[s * TILE : (s + 1) * TILE, :]
        return lax.dot_general(x_ref[...], ys, NT, preferred_element_type=F32) * scale

    @pl.when(fast)
    def _():
        v_ref[...] = jnp.exp2(c_bits - top_c + SHIFT)
        for s in range(slabs):
            power = jnp.exp2(scores(s))
            m_ref[s][...] = power
            total = None if s == 0 else acc_ref[...]
            for k in range(TILE // LANES):
                row = s * (TILE // LANES) + k
                term = power[:, k * LANES : (k + 1) * LANES] * v_ref[row : row + 1, :]
                total = term if total is None else total + term
            acc_ref[...] = total
        top_ref[...] = jnp.broadcast_to(top_c - SHIFT, top_ref.shape)

    @pl.when(jnp.logical_not(fast))
    def _():
        v_ref[...] = c_bits
        for s in range(slabs):
            m_ref[s][...] = scores(s)
        careful_rows(m_ref, False, v_ref, acc_ref, top_ref, 0)

    row_ref[...] = before_ref[...]
    for d in range(blocks):
        here = slice(d * LANES, (d + 1) * LANES)
        total = log2(lane_sums(acc_ref[here, :])) + top_ref[here, :].T[0:1, :]
        row_ref[pl.ds(holder(g * blocks + d, blocks, before_ref.shape[0] // blocks), 1), :] = total
    out_ref[...] = row_ref[...] if out_ref.ndim == 2 else jnp.broadcast_to(row_ref[...][None], out_ref.shape)


def row_kernel(log_ends, m_ref, bounds, got_ref, out_ref, v_ref, acc_ref, top_ref, row_ref):
    slabs = len(m_ref) // len(bounds)
    rows = m_ref[0].shape[0]
    fast = all_fast(bounds)
    c_bits = log_ends - combine(got_ref[...])
    top_c = jnp.max(c_bits, keepdims=True)
    total_rows = rows * len(bounds)

    @pl.when(fast)
    def _():
        v_ref[...] = jnp.exp2(c_bits - top_c + SHIFT)
        for g in range(len(bounds)):
            fast_rows(m_ref[g * slabs : (g + 1) * slabs], v_ref, acc_ref, g * rows)
        for b in range(total_rows // LANES):
            row_ref[pl.ds(holder(b, rows // LANES, len(bounds)), 1), :] = lane_sums(acc_ref[b * LANES : (b + 1) * LANES, :])
        row_ref[...] = log2(row_ref[...]) + (top_c - SHIFT)

    @pl.when(jnp.logical_not(fast))
    def _():
        v_ref[...] = c_bits
        for g in range(len(bounds)):
            careful_rows(m_ref[g * slabs : (g + 1) * slabs], is_fast(bounds[g]), v_ref, acc_ref, top_ref, g * rows)
        for b in range(total_rows // LANES):
            here = slice(b * LANES, (b + 1) * LANES)
            row_ref[pl.ds(holder(b, rows // LANES, len(bounds)), 1), :] = log2(lane_sums(acc_ref[here, :])) + top_ref[here, :].T[0:1, :]

    out_ref[...] = jnp.broadcast_to(row_ref[...][None], out_ref.shape)


def col_kernel(log_cells, m_ref, bounds, got_ref, out_ref, u_ref, f_ref, sum_ref):
    slabs = len(m_ref) // len(bounds)
    rows = m_ref[0].shape[0]
    fast = all_fast(bounds)
    f_bits = log_cells - combine(got_ref[...])
    top_f = jnp.max(f_bits, keepdims=True)
    step = 64
    n = slabs * (TILE // LANES)

    def place():
        for b in range(rows * len(bounds) // LANES):
            spread(f_ref[pl.ds(holder(b, rows // LANES, len(bounds)), 1), :], u_ref, b * LANES)

    @pl.when(fast)
    def _():
        f_ref[...] = jnp.exp2(f_bits - top_f + SHIFT)
        place()
        totals = (jnp.zeros((8, LANES), F32),) * n
        for g in range(len(bounds)):

            def body(r, totals):
                here = pl.ds(pl.multiple_of(r * step, step), step)
                u = u_ref[pl.ds(pl.multiple_of(g * rows + r * step, step), step), :]
                new = []
                for s in range(slabs):
                    for k in range(TILE // LANES):
                        term = m_ref[g * slabs + s][here, k * LANES : (k + 1) * LANES] * u
                        total = totals[len(new)]
                        for part in range(step // 8):
                            total = total + term[part * 8 : (part + 1) * 8, :]
                        new.append(total)
                return tuple(new)

            totals = lax.fori_loop(0, rows // step, body, totals, unroll=2)
        for k in range(n):
            sum_ref[k : k + 1, :] = jnp.sum(totals[k], axis=0, keepdims=True)
        sum_ref[...] = log2(sum_ref[...]) + (top_f - SHIFT)

    @pl.when(jnp.logical_not(fast))
    def _():
        f_ref[...] = f_bits
        place()
        step = 16
        for s in range(slabs):

            def score(g, r):
                here = pl.ds(pl.multiple_of(r * step, step), step)
                u = u_ref[pl.ds(pl.multiple_of(g * rows + r * step, step), step), :]
                u = jnp.concatenate([u] * (TILE // LANES), axis=1)
                return score_of(is_fast(bounds[g]), m_ref[g * slabs + s][here, :]) + u

            def over(one, carry):
                for g in range(len(bounds)):
                    carry = lax.fori_loop(0, rows // step, functools.partial(one, g), carry)
                return carry

            def most(g, r, top):
                return jnp.maximum(top, score(g, r))

            top = jnp.max(over(most, jnp.full((step, TILE), -3.0e38, F32)), axis=0, keepdims=True)

            def add(g, r, total):
                return total + jnp.exp2(score(g, r) - top)

            total = jnp.sum(over(add, jnp.zeros((step, TILE), F32)), axis=0, keepdims=True)
            total = log2(total) + top
            for k in range(TILE // LANES):
                row = s * (TILE // LANES) + k
                sum_ref[row : row + 1, :] = total[:, k * LANES : (k + 1) * LANES]

    out_ref[...] = jnp.broadcast_to(sum_ref[...][None], out_ref.shape)


def last_kernel(g, log_cells, log_ends, m_ref, bounds, xnorms, rows_ref, cols_ref, y_ref, ynorm_ref, before_ref,
                out_ref, after_ref, *rest):
    *pots, f_ref, u_ref, v_ref, mass_ref, row_ref = rest
    slabs = len(m_ref)
    rows, depth = m_ref[0].shape[0], y_ref.shape[1]
    blocks = rows // LANES
    fast = all_fast(bounds)
    f_bits = log_cells - combine(rows_ref[...])
    c_bits = log_ends - combine(cols_ref[...])
    top_f = jnp.max(f_bits, keepdims=True) - 24.0

    def weigh(here, weight):
        u = u_ref[here, :]
        moved = None
        mass = None
        for s in range(slabs):
            parts = []
            for k in range(TILE // LANES):
                row = s * (TILE // LANES) + k
                part = weight(m_ref[s][here, k * LANES : (k + 1) * LANES], u, v_ref[row : row + 1, :])
                mass = part if mass is None else mass + part
                parts.append(part.astype(BF16))
            term = jnp.dot(jnp.concatenate(parts, axis=1), y_ref[s * TILE : (s + 1) * TILE, :], preferred_element_type=F32)
            moved = term if moved is None else moved + term
        mass_ref[here, :] = mass
        out_ref[here, :] = moved.astype(out_ref.dtype)

    def place():
        for d in range(blocks):
            spread(f_ref[pl.ds(holder(g * blocks + d, blocks, len(bounds)), 1), :], u_ref, d * LANES)

    @pl.when(fast)
    def _():
        f_ref[...] = jnp.exp2(f_bits - top_f)
        v_ref[...] = jnp.exp2(c_bits + (top_f - log_cells))
        place()
        weigh(slice(0, rows), lambda m, u, v: (m * u) * v)

    @pl.when(jnp.logical_not(fast))
    def _():
        f_ref[...] = f_bits
        v_ref[...] = c_bits - log_cells
        place()
        mine = is_fast(bounds[g])
        step = 64

        def body(r, carry):
            here = pl.ds(pl.multiple_of(r * step, step), step)
            weigh(here, lambda m, u, v: jnp.exp2((score_of(mine, m) + u) + v))
            return carry

        lax.fori_loop(0, rows // step, body, 0)

    row_ref[...] = jnp.zeros_like(row_ref)
    for d in range(blocks):
        row_ref[d : d + 1, :] = lane_sums(mass_ref[d * LANES : (d + 1) * LANES, :])
    mass = row_ref[...]
    if out_ref.dtype == F32:
        out_ref[rows : rows + 8, :] = jnp.concatenate([mass, mass], axis=1)
    else:
        high = mass.astype(BF16).astype(F32)
        mid = (mass - high).astype(BF16).astype(F32)
        low = mass - high - mid
        first = jnp.concatenate([high, mid], axis=1)
        second = jnp.concatenate([low, low], axis=1)
        out_ref[rows : rows + 16, :] = jnp.concatenate([first, second], axis=0).astype(BF16)
    after_ref[...] = before_ref[...]
    if pots:
        end_ref, cell_ref = pots
        for p, xnorm_ref in enumerate(xnorms):
            for d in range(blocks):
                f_ref[pl.ds(holder(p * blocks + d, blocks, len(bounds)), 1), :] = xnorm_ref[d : d + 1, :]
        end_ref[...] = f_bits * (EPS / LOG2E) + f_ref[...] * (1.0 / depth)
        cell_ref[...] = c_bits * (EPS / LOG2E) + ynorm_ref[...] * (1.0 / depth)


def sum_kernel(own_ref, got_refs, out_refs):
    rows = own_ref.shape[0] - 8
    mass = own_ref[rows : rows + 8, :LANES]
    for got_ref in got_refs:
        parts = got_ref[rows : rows + 16, :].astype(F32)
        mass = mass + ((parts[0:8, :LANES] + parts[0:8, LANES:]) + parts[8:16, :LANES])
    wide = jnp.concatenate([mass, mass], axis=1)
    for d, out_ref in enumerate(out_refs):
        here = slice(d * LANES, (d + 1) * LANES)
        total = own_ref[here, :]
        for got_ref in got_refs:
            total = total + got_ref[here, :].astype(F32)
        out_ref[0:LANES, :] = total
        out_ref[LANES : LANES + 8, :] = jnp.broadcast_to(wide[d : d + 1, :], (8, wide.shape[1]))


def end_kernel(x_ref, got_refs, out_ref):
    total = functools.reduce(jnp.add, [got_ref[...] for got_ref in got_refs])
    wide = jnp.broadcast_to(total[LANES : LANES + 1, :LANES], (LANES, LANES)).T
    x = x_ref[...].astype(F32)
    out_ref[:, :LANES] = x[:, :LANES] * wide - total[:LANES, :LANES]
    out_ref[:, LANES:] = x[:, LANES:] * wide - total[:LANES, LANES:]


def grouped(kernel, at, *counts):
    def body(*refs):
        groups, n = [], at
        for count in counts:
            groups.append(refs[n : n + count] if count else refs[n])
            n += max(count, 1)
        kernel(*refs[:at], *groups, *refs[n:])

    body.__name__ = getattr(kernel, "func", kernel).__name__
    return body


def call(kernel, outs, scratch, limit_mib=16, cost=None):
    return pl.pallas_call(
        kernel,
        name=getattr(kernel, "func", kernel).__name__,
        out_shape=outs,
        cost_estimate=cost,
        scratch_shapes=[pltpu.VMEM(s, F32) for s in scratch],
        compiler_params=pltpu.CompilerParams(vmem_limit_bytes=limit_mib << 20),
    )


def swap(parts, axis):
    return lax.all_to_all(parts, axis, 0, 0, tiled=True)


def flip(value, by, turned):
    n_row, n_col = lax.axis_size("row"), lax.axis_size("col")
    pairs = [(r * n_col + n, r * n_col + (n ^ (turned if r % 2 else by))) for r in range(n_row) for n in range(n_col)]
    return lax.ppermute(value, ("row", "col"), pairs)


def pin(m):
    return pltpu.with_memory_space_constraint(m, pltpu.VMEM)


def inside(*shape, dtype=F32):
    return pltpu.VMEM(shape, dtype)


def shards(endpoints, cells):
    n_row, n_col = lax.axis_size("row"), lax.axis_size("col")
    nx = 1 << ((n_col.bit_length() - 1) // 2)
    ny = n_col // nx
    square = nx == ny

    def between(value, d):
        return flip(value, d, d * ny if square else d)

    def across(value, g):
        return flip(value, g * nx, g if square else g * nx)

    own, depth = endpoints.shape
    rows, cols, part = own * n_col, cells.shape[0], own * nx
    log_cells = math.log2(cols * n_col)
    log_ends = math.log2(rows * n_row)
    rb, cb, slabs = rows // LANES, cols // LANES, cols // TILE
    order = sorted(range(1, ny), key=lambda g: min(g, ny - g))
    work = 2 * part * cols * depth
    small = pl.CostEstimate(flops=work // 16, bytes_accessed=part * cols // 4, transcendentals=0)
    cost = pl.CostEstimate(flops=work, bytes_accessed=4 * part * cols, transcendentals=0)

    ynorm = call(cells_kernel, inside(cb, LANES), [], cost=cost)(pin(cells))
    near, sums = call(
        grouped(join_kernel, 1, nx),
        [inside(part, depth, dtype=BF16), inside(rb, LANES)],
        [],
    )(pin(ynorm), *[pin(between(endpoints, d)) if d else endpoints for d in range(nx)])
    x = [near] + [across(near, g) for g in range(1, ny)]

    m, bounds, xnorms = [None] * ny, [None] * ny, [None] * ny
    for g in [0] + order:
        out = inside(n_col, rb, LANES) if g == order[-1] else inside(rb, LANES)
        *m[g], bounds[g], xnorms[g], sums = call(
            grouped(functools.partial(first_kernel, g), 4, slabs),
            [inside(part, TILE)] * slabs + [inside(8, LANES), inside(8, LANES), out],
            [(cb, LANES), (part, LANES), (part, LANES), (rb, LANES)],
            cost=cost,
        )(pin(x[g]), pin(cells), pin(ynorm), pin(sums))
    block = [pin(slab) for g in range(ny) for slab in m[g]]
    flags = [pin(bound) for bound in bounds]

    for step in range(ITERS):
        if step > 0:
            sums = call(
                grouped(functools.partial(row_kernel, log_ends), 0, ny * slabs, ny),
                inside(n_col, rb, LANES),
                [(cb, LANES), (rows, LANES), (rows, LANES), (rb, LANES)],
            )(*block, *flags, pin(got_cols))
        got_rows = swap(sums, "col")
        sums = call(
            grouped(functools.partial(col_kernel, log_cells), 0, ny * slabs, ny),
            inside(n_row, cb, LANES),
            [(rows, LANES), (rb, LANES), (cb, LANES)],
        )(*block, *flags, pin(got_rows))
        got_cols = swap(sums, "row")

    token = inside(8, LANES)
    sent, after = [], bounds[0]
    for g in order[::-1] + [0]:
        message = inside(part + 16, depth, dtype=BF16) if g else inside(part + 8, depth)
        pots = [] if g else [jax.ShapeDtypeStruct((rb, LANES), F32), jax.ShapeDtypeStruct((cb, LANES), F32)]
        message, after, *pots = call(
            grouped(functools.partial(last_kernel, g, log_cells, log_ends), 0, slabs, ny, ny),
            [message, token] + pots,
            [(rb, LANES), (part, LANES), (cb, LANES), (part, LANES), (8, LANES)],
            cost=small,
        )(*map(pin, m[g]), *flags, *map(pin, xnorms), pin(got_rows), pin(got_cols), pin(cells), pin(ynorm), pin(after))
        sent.append(across(message, g) if g else message)
    end_pot, cell_pot = pots
    sums = call(
        grouped(sum_kernel, 0, 0, ny - 1, nx),
        [inside(own + 8, depth)] * nx,
        [],
    )(pin(sent[-1]), *map(pin, sent[:-1]))
    sums = [sums[0]] + [between(sums[d], d) for d in range(1, nx)]
    displacement = call(
        grouped(end_kernel, 1, nx),
        jax.ShapeDtypeStruct((own, depth), F32),
        [],
    )(endpoints, *map(pin, sums))
    return end_pot.reshape(rows), cell_pot.reshape(cols), displacement


def solution(mesh):
    return jax.shard_map(
        shards,
        mesh=mesh,
        in_specs=(P(("row", "col"), None), P("col", None)),
        out_specs=(P("row"), P("col"), P(("row", "col"), None)),
        check_vma=False,
    )
```

```python
import functools
import math

import jax
import jax.numpy as jnp
from jax import lax
from jax.experimental import pallas as pl
from jax.experimental.pallas import tpu as pltpu
from jax.sharding import PartitionSpec as P

ITERS = 3
EPS = 0.1
LOG2E = math.log2(math.e)
LIMIT = 52.0
SHIFT = 50.0
LANES = 128
TILE = 512
F32 = jnp.float32
BF16 = jnp.bfloat16
NT = (((1,), (1,)), ((), ()))


def log2(x):
    return jnp.log(x) * LOG2E


def combine(parts):
    top = jnp.max(parts, axis=0)
    return top + log2(jnp.sum(jnp.exp2(parts - top[None]), axis=0))


def norms(src_ref, out_ref):
    rows, depth = src_ref.shape
    step = min(TILE, rows)
    ones = jnp.ones((8, depth), BF16)
    for t in range(rows // step):
        val = src_ref[t * step : (t + 1) * step, :].astype(F32)
        sq = val * val
        high = sq.astype(BF16)
        low = (sq - high.astype(F32)).astype(BF16)
        got = lax.dot_general(ones, high, NT, preferred_element_type=F32)
        got = got + lax.dot_general(ones, low, NT, preferred_element_type=F32)
        for k in range(step // LANES):
            row = t * (step // LANES) + k
            out_ref[row : row + 1, :] = got[0:1, k * LANES : (k + 1) * LANES]


def holder(b, nx, ny):
    g, d = divmod(b, nx)
    turned = d * ny + g if nx == ny else b
    odd = lax.rem(lax.axis_index("row"), 2) == 1
    return lax.axis_index("col") ^ jnp.where(odd, turned, b)


def spread(row, out_ref, at):
    out_ref[at : at + LANES, :] = jnp.broadcast_to(row, (LANES, LANES)).T


def lane_sums(block):
    return jnp.sum(block.T, axis=0, keepdims=True)


def is_fast(bound_ref):
    return jnp.max(bound_ref[0:1, :]) <= LIMIT


def all_fast(bounds):
    return jnp.max(functools.reduce(jnp.maximum, [b[0:1, :] for b in bounds])) <= LIMIT


def score_of(fast, m):
    return jnp.where(fast, log2(m), m)


def careful_rows(slabs, fast, c_ref, acc_ref, top_ref, at):
    step = 64

    def body(r, carry):
        here = pl.ds(pl.multiple_of(r * step, step), step)
        there = pl.ds(pl.multiple_of(at + r * step, step), step)

        def score(s, k):
            row = s * (TILE // LANES) + k
            return score_of(fast, slabs[s][here, k * LANES : (k + 1) * LANES]) + c_ref[row : row + 1, :]

        each = [(s, k) for s in range(len(slabs)) for k in range(TILE // LANES)]
        top = functools.reduce(jnp.maximum, [score(s, k) for s, k in each])
        top = jnp.broadcast_to(jnp.max(top, axis=1, keepdims=True), top.shape)
        acc_ref[there, :] = functools.reduce(jnp.add, [jnp.exp2(score(s, k) - top) for s, k in each])
        top_ref[there, :] = top
        return carry

    lax.fori_loop(0, slabs[0].shape[0] // step, body, 0)


def fast_rows(slabs, v_ref, acc_ref, at):
    step = min(256, slabs[0].shape[0])
    for r in range(slabs[0].shape[0] // step):
        total = None
        for s in range(len(slabs)):
            for k in range(TILE // LANES):
                row = s * (TILE // LANES) + k
                term = slabs[s][r * step : (r + 1) * step, k * LANES : (k + 1) * LANES] * v_ref[row : row + 1, :]
                total = term if total is None else total + term
        acc_ref[at + r * step : at + (r + 1) * step, :] = total


def cells_kernel(y_ref, ynorm_ref):
    norms(y_ref, ynorm_ref)


def join_kernel(ynorm_ref, got_refs, out_ref, start_ref):
    for d, got_ref in enumerate(got_refs):
        out_ref[d * LANES : (d + 1) * LANES, :] = got_ref[...]
    start_ref[...] = ynorm_ref[0 : start_ref.shape[0], :]


def first_kernel(g, x_ref, y_ref, ynorm_ref, before_ref, m_ref, bound_ref, xnorm_ref, out_ref,
                 v_ref, acc_ref, top_ref, row_ref):
    rows, depth = x_ref.shape
    blocks = rows // LANES
    slabs = len(m_ref)
    scale = 2.0 * LOG2E / (EPS * depth)
    norms(x_ref, xnorm_ref)
    most_x = jnp.max(xnorm_ref[0:blocks, :], keepdims=True)
    most_y = jnp.max(ynorm_ref[...], keepdims=True)
    bound = scale * jnp.sqrt(most_x * most_y)
    bound_ref[...] = jnp.broadcast_to(bound, bound_ref.shape)
    fast = jnp.max(bound) <= LIMIT
    c_bits = ynorm_ref[...] * (-LOG2E / (EPS * depth))
    top_c = jnp.max(c_bits, keepdims=True)

    def scores(s):
        ys = y_ref[s * TILE : (s + 1) * TILE, :]
        return lax.dot_general(x_ref[...], ys, NT, preferred_element_type=F32) * scale

    @pl.when(fast)
    def _():
        v_ref[...] = jnp.exp2(c_bits - top_c + SHIFT)
        for s in range(slabs):
            power = jnp.exp2(scores(s))
            m_ref[s][...] = power
            total = None if s == 0 else acc_ref[...]
            for k in range(TILE // LANES):
                row = s * (TILE // LANES) + k
                term = power[:, k * LANES : (k + 1) * LANES] * v_ref[row : row + 1, :]
                total = term if total is None else total + term
            acc_ref[...] = total
        top_ref[...] = jnp.broadcast_to(top_c - SHIFT, top_ref.shape)

    @pl.when(jnp.logical_not(fast))
    def _():
        v_ref[...] = c_bits
        for s in range(slabs):
            m_ref[s][...] = scores(s)
        careful_rows(m_ref, False, v_ref, acc_ref, top_ref, 0)

    row_ref[...] = before_ref[...]
    for d in range(blocks):
        here = slice(d * LANES, (d + 1) * LANES)
        total = log2(lane_sums(acc_ref[here, :])) + top_ref[here, :].T[0:1, :]
        row_ref[pl.ds(holder(g * blocks + d, blocks, before_ref.shape[0] // blocks), 1), :] = total
    out_ref[...] = row_ref[...] if out_ref.ndim == 2 else jnp.broadcast_to(row_ref[...][None], out_ref.shape)


def row_kernel(log_ends, m_ref, bounds, got_ref, out_ref, v_ref, acc_ref, top_ref, row_ref):
    slabs = len(m_ref) // len(bounds)
    rows = m_ref[0].shape[0]
    fast = all_fast(bounds)
    c_bits = log_ends - combine(got_ref[...])
    top_c = jnp.max(c_bits, keepdims=True)
    total_rows = rows * len(bounds)

    @pl.when(fast)
    def _():
        v_ref[...] = jnp.exp2(c_bits - top_c + SHIFT)
        for g in range(len(bounds)):
            fast_rows(m_ref[g * slabs : (g + 1) * slabs], v_ref, acc_ref, g * rows)
        for b in range(total_rows // LANES):
            row_ref[pl.ds(holder(b, rows // LANES, len(bounds)), 1), :] = lane_sums(acc_ref[b * LANES : (b + 1) * LANES, :])
        row_ref[...] = log2(row_ref[...]) + (top_c - SHIFT)

    @pl.when(jnp.logical_not(fast))
    def _():
        v_ref[...] = c_bits
        for g in range(len(bounds)):
            careful_rows(m_ref[g * slabs : (g + 1) * slabs], is_fast(bounds[g]), v_ref, acc_ref, top_ref, g * rows)
        for b in range(total_rows // LANES):
            here = slice(b * LANES, (b + 1) * LANES)
            row_ref[pl.ds(holder(b, rows // LANES, len(bounds)), 1), :] = log2(lane_sums(acc_ref[here, :])) + top_ref[here, :].T[0:1, :]

    out_ref[...] = jnp.broadcast_to(row_ref[...][None], out_ref.shape)


def col_kernel(log_cells, m_ref, bounds, got_ref, out_ref, u_ref, f_ref, sum_ref):
    slabs = len(m_ref) // len(bounds)
    rows = m_ref[0].shape[0]
    fast = all_fast(bounds)
    f_bits = log_cells - combine(got_ref[...])
    top_f = jnp.max(f_bits, keepdims=True)
    step = 64
    n = slabs * (TILE // LANES)

    def place():
        for b in range(rows * len(bounds) // LANES):
            spread(f_ref[pl.ds(holder(b, rows // LANES, len(bounds)), 1), :], u_ref, b * LANES)

    @pl.when(fast)
    def _():
        f_ref[...] = jnp.exp2(f_bits - top_f + SHIFT)
        place()
        totals = (jnp.zeros((8, LANES), F32),) * n
        for g in range(len(bounds)):

            def body(r, totals):
                here = pl.ds(pl.multiple_of(r * step, step), step)
                u = u_ref[pl.ds(pl.multiple_of(g * rows + r * step, step), step), :]
                new = []
                for s in range(slabs):
                    for k in range(TILE // LANES):
                        term = m_ref[g * slabs + s][here, k * LANES : (k + 1) * LANES] * u
                        total = totals[len(new)]
                        for part in range(step // 8):
                            total = total + term[part * 8 : (part + 1) * 8, :]
                        new.append(total)
                return tuple(new)

            totals = lax.fori_loop(0, rows // step, body, totals, unroll=2)
        for k in range(n):
            sum_ref[k : k + 1, :] = jnp.sum(totals[k], axis=0, keepdims=True)
        sum_ref[...] = log2(sum_ref[...]) + (top_f - SHIFT)

    @pl.when(jnp.logical_not(fast))
    def _():
        f_ref[...] = f_bits
        place()
        step = 16
        for s in range(slabs):

            def score(g, r):
                here = pl.ds(pl.multiple_of(r * step, step), step)
                u = u_ref[pl.ds(pl.multiple_of(g * rows + r * step, step), step), :]
                u = jnp.concatenate([u] * (TILE // LANES), axis=1)
                return score_of(is_fast(bounds[g]), m_ref[g * slabs + s][here, :]) + u

            def over(one, carry):
                for g in range(len(bounds)):
                    carry = lax.fori_loop(0, rows // step, functools.partial(one, g), carry)
                return carry

            def most(g, r, top):
                return jnp.maximum(top, score(g, r))

            top = jnp.max(over(most, jnp.full((step, TILE), -3.0e38, F32)), axis=0, keepdims=True)

            def add(g, r, total):
                return total + jnp.exp2(score(g, r) - top)

            total = jnp.sum(over(add, jnp.zeros((step, TILE), F32)), axis=0, keepdims=True)
            total = log2(total) + top
            for k in range(TILE // LANES):
                row = s * (TILE // LANES) + k
                sum_ref[row : row + 1, :] = total[:, k * LANES : (k + 1) * LANES]

    out_ref[...] = jnp.broadcast_to(sum_ref[...][None], out_ref.shape)


def last_kernel(log_cells, log_ends, m_ref, bounds, xnorms, rows_ref, cols_ref, y_ref, ynorm_ref,
                end_ref, cell_ref, out_ref, f_ref, u_ref, v_ref, mass_ref):
    parts = len(bounds)
    slabs = len(m_ref) // parts
    rows = m_ref[0].shape[0]
    blocks = rows // LANES
    fast = all_fast(bounds)
    f_bits = log_cells - combine(rows_ref[...])
    c_bits = log_ends - combine(cols_ref[...])
    top_f = jnp.max(f_bits, keepdims=True) - 24.0
    for g in range(parts):
        for d in range(blocks):
            f_ref[pl.ds(holder(g * blocks + d, blocks, parts), 1), :] = xnorms[g][d : d + 1, :]
    end_ref[...] = f_bits * (EPS / LOG2E) + f_ref[...] * (1.0 / y_ref.shape[1])
    cell_ref[...] = c_bits * (EPS / LOG2E) + ynorm_ref[...] * (1.0 / y_ref.shape[1])

    def place():
        for b in range(parts * blocks):
            spread(f_ref[pl.ds(holder(b, blocks, parts), 1), :], u_ref, b * LANES)

    def weigh(some, here, size, weight):
        at = [g * rows + (here.start if isinstance(here, slice) else here) for g in some]
        us = [u_ref[pl.ds(a, size), :] for a in at]
        moved, mass = None, None
        for s in range(slabs):
            columns = []
            for k in range(TILE // LANES):
                row = s * (TILE // LANES) + k
                v = v_ref[row : row + 1, :]
                wide = slice(k * LANES, (k + 1) * LANES)
                where = pl.ds(here.start if isinstance(here, slice) else here, size)
                each = [weight(g, m_ref[g * slabs + s][where, wide], u, v) for g, u in zip(some, us)]
                mass = each if mass is None else [a + b for a, b in zip(mass, each)]
                columns.append(jnp.concatenate([one.astype(BF16) for one in each], axis=0))
            term = jnp.dot(jnp.concatenate(columns, axis=1), y_ref[s * TILE : (s + 1) * TILE, :], preferred_element_type=F32)
            moved = term if moved is None else moved + term
        for a, one in zip(at, mass):
            mass_ref[pl.ds(a, size), :] = one
        return moved.astype(BF16)

    @pl.when(fast)
    def _():
        f_ref[...] = jnp.exp2(f_bits - top_f)
        v_ref[...] = jnp.exp2(c_bits + (top_f - log_cells))
        place()
        for p in range(0, parts, 2):
            moved = weigh((p, p + 1), slice(0, rows), rows, lambda g, m, u, v: (m * u) * v)
            for b in range(2 * blocks):
                out_ref[holder(p * blocks + b, blocks, parts), 0:LANES, :] = moved[b * LANES : (b + 1) * LANES, :]

    @pl.when(jnp.logical_not(fast))
    def _():
        f_ref[...] = f_bits
        v_ref[...] = c_bits - log_cells
        place()
        step = 64
        for g in range(parts):
            mine = is_fast(bounds[g])
            for d in range(blocks):

                def body(r, carry):
                    here = pl.multiple_of(d * LANES + r * step, step)
                    moved = weigh((g,), here, step, lambda _, m, u, v: jnp.exp2((score_of(mine, m) + u) + v))
                    out_ref[holder(g * blocks + d, blocks, parts), pl.ds(pl.multiple_of(r * step, step), step), :] = moved
                    return carry

                lax.fori_loop(0, LANES // step, body, 0)

    for b in range(parts * blocks):
        mass = jnp.broadcast_to(lane_sums(mass_ref[b * LANES : (b + 1) * LANES, :]), (8, LANES))
        high = mass.astype(BF16).astype(F32)
        mid = (mass - high).astype(BF16).astype(F32)
        low = mass - high - mid
        first = jnp.concatenate([high, mid], axis=1)
        second = jnp.concatenate([low, low], axis=1)
        out_ref[holder(b, blocks, parts), LANES : LANES + 16, :] = jnp.concatenate([first, second], axis=0).astype(BF16)


def end_kernel(got_ref, x_ref, out_ref):
    moved, mass = None, None
    for n in range(got_ref.shape[0]):
        part = got_ref[n, 0:LANES, :].astype(F32)
        parts = got_ref[n, LANES : LANES + 16, :].astype(F32)
        weight = (parts[0:1, :LANES] + parts[0:1, LANES:]) + parts[8:9, :LANES]
        moved = part if moved is None else moved + part
        mass = weight if mass is None else mass + weight
    wide = jnp.broadcast_to(mass, (LANES, LANES)).T
    x = x_ref[...].astype(F32)
    out_ref[:, :LANES] = x[:, :LANES] * wide - moved[:, :LANES]
    out_ref[:, LANES:] = x[:, LANES:] * wide - moved[:, LANES:]


def grouped(kernel, at, *counts):
    def body(*refs):
        groups, n = [], at
        for count in counts:
            groups.append(refs[n : n + count] if count else refs[n])
            n += max(count, 1)
        kernel(*refs[:at], *groups, *refs[n:])

    body.__name__ = getattr(kernel, "func", kernel).__name__
    return body


def call(kernel, outs, scratch, limit_mib=16, cost=None):
    return pl.pallas_call(
        kernel,
        name=getattr(kernel, "func", kernel).__name__,
        out_shape=outs,
        cost_estimate=cost,
        scratch_shapes=[pltpu.VMEM(s, F32) for s in scratch],
        compiler_params=pltpu.CompilerParams(vmem_limit_bytes=limit_mib << 20),
    )


def swap(parts, axis):
    return lax.all_to_all(parts, axis, 0, 0, tiled=True)


def flip(value, by, turned):
    n_row, n_col = lax.axis_size("row"), lax.axis_size("col")
    pairs = [(r * n_col + n, r * n_col + (n ^ (turned if r % 2 else by))) for r in range(n_row) for n in range(n_col)]
    return lax.ppermute(value, ("row", "col"), pairs)


def pin(m):
    return pltpu.with_memory_space_constraint(m, pltpu.VMEM)


def inside(*shape, dtype=F32):
    return pltpu.VMEM(shape, dtype)


def shards(endpoints, cells):
    n_row, n_col = lax.axis_size("row"), lax.axis_size("col")
    nx = 1 << ((n_col.bit_length() - 1) // 2)
    ny = n_col // nx
    square = nx == ny

    def between(value, d):
        return flip(value, d, d * ny if square else d)

    def across(value, g):
        return flip(value, g * nx, g if square else g * nx)

    own, depth = endpoints.shape
    rows, cols, part = own * n_col, cells.shape[0], own * nx
    log_cells = math.log2(cols * n_col)
    log_ends = math.log2(rows * n_row)
    rb, cb, slabs = rows // LANES, cols // LANES, cols // TILE
    order = sorted(range(1, ny), key=lambda g: min(g, ny - g))
    work = 2 * part * cols * depth
    cost = pl.CostEstimate(flops=work, bytes_accessed=4 * part * cols, transcendentals=0)

    ynorm = call(cells_kernel, inside(cb, LANES), [], cost=cost)(pin(cells))
    near, sums = call(
        grouped(join_kernel, 1, nx),
        [inside(part, depth, dtype=BF16), inside(rb, LANES)],
        [],
    )(pin(ynorm), *[pin(between(endpoints, d)) if d else endpoints for d in range(nx)])
    x = [near] + [across(near, g) for g in range(1, ny)]

    m, bounds, xnorms = [None] * ny, [None] * ny, [None] * ny
    for g in [0] + order:
        out = inside(n_col, rb, LANES) if g == order[-1] else inside(rb, LANES)
        *m[g], bounds[g], xnorms[g], sums = call(
            grouped(functools.partial(first_kernel, g), 4, slabs),
            [inside(part, TILE)] * slabs + [inside(8, LANES), inside(8, LANES), out],
            [(cb, LANES), (part, LANES), (part, LANES), (rb, LANES)],
            cost=cost,
        )(pin(x[g]), pin(cells), pin(ynorm), pin(sums))
    block = [pin(slab) for g in range(ny) for slab in m[g]]
    flags = [pin(bound) for bound in bounds]

    for step in range(ITERS):
        if step > 0:
            sums = call(
                grouped(functools.partial(row_kernel, log_ends), 0, ny * slabs, ny),
                inside(n_col, rb, LANES),
                [(cb, LANES), (rows, LANES), (rows, LANES), (rb, LANES)],
            )(*block, *flags, pin(got_cols))
        got_rows = swap(sums, "col")
        sums = call(
            grouped(functools.partial(col_kernel, log_cells), 0, ny * slabs, ny),
            inside(n_row, cb, LANES),
            [(rows, LANES), (rb, LANES), (cb, LANES)],
        )(*block, *flags, pin(got_rows))
        got_cols = swap(sums, "row")

    end_pot, cell_pot, moved = call(
        grouped(functools.partial(last_kernel, log_cells, log_ends), 0, ny * slabs, ny, ny),
        [jax.ShapeDtypeStruct((rb, LANES), F32), jax.ShapeDtypeStruct((cb, LANES), F32), inside(n_col, own + 16, depth, dtype=BF16)],
        [(rb, LANES), (rows, LANES), (cb, LANES), (rows, LANES)],
        limit_mib=14,
    )(*block, *flags, *map(pin, xnorms), pin(got_rows), pin(got_cols), pin(cells), pin(ynorm))
    displacement = call(end_kernel, jax.ShapeDtypeStruct((own, depth), F32), [])(pin(swap(moved, "col")), endpoints)
    return end_pot.reshape(rows), cell_pot.reshape(cols), displacement


def solution(mesh):
    return jax.shard_map(
        shards,
        mesh=mesh,
        in_specs=(P(("row", "col"), None), P("col", None)),
        out_specs=(P("row"), P("col"), P(("row", "col"), None)),
        check_vma=False,
    )
```

```python
import functools
import math

import jax
import jax.numpy as jnp
from jax import lax
from jax.experimental import pallas as pl
from jax.experimental.pallas import tpu as pltpu
from jax.sharding import PartitionSpec as P

ITERS = 3
EPS = 0.1
LOG2E = math.log2(math.e)
LIMIT = 52.0
SHIFT = 50.0
LANES = 128
TILE = 512
F32 = jnp.float32
BF16 = jnp.bfloat16
NT = (((1,), (1,)), ((), ()))


def log2(x):
    return jnp.log(x) * LOG2E


def combine(parts):
    top = jnp.max(parts, axis=0)
    return top + log2(jnp.sum(jnp.exp2(parts - top[None]), axis=0))


def fast_of(bound_ref):
    return jnp.max(bound_ref[0:1, :]) <= LIMIT


def norms(src_ref, out_ref):
    rows, depth = src_ref.shape
    step = min(TILE, rows)
    ones = jnp.ones((8, depth), BF16)
    for t in range(rows // step):
        val = src_ref[t * step : (t + 1) * step, :].astype(F32)
        sq = val * val
        high = sq.astype(BF16)
        low = (sq - high.astype(F32)).astype(BF16)
        got = lax.dot_general(ones, high, NT, preferred_element_type=F32)
        got = got + lax.dot_general(ones, low, NT, preferred_element_type=F32)
        for k in range(step // LANES):
            row = t * (step // LANES) + k
            out_ref[row : row + 1, :] = got[0:1, k * LANES : (k + 1) * LANES]


def spread(rows, out_ref):
    for b in range(rows.shape[0]):
        out_ref[b * LANES : (b + 1) * LANES, :] = jnp.broadcast_to(rows[b : b + 1, :], (LANES, LANES)).T


def gather_rows(src_ref, out_ref):
    for b in range(src_ref.shape[0] // LANES):
        block = src_ref[b * LANES : (b + 1) * LANES, :].T
        out_ref[b : b + 1, :] = jnp.sum(block, axis=0, keepdims=True)


def first_rows(src_ref, out_ref):
    for b in range(src_ref.shape[0] // LANES):
        block = src_ref[b * LANES : (b + 1) * LANES, :].T
        out_ref[b : b + 1, :] = block[0:1, :]


def careful_rows(m_ref, c_ref, acc_ref, top_ref):
    slabs, rows = len(m_ref), m_ref[0].shape[0]
    step = 64

    def body(r, carry):
        here = pl.ds(pl.multiple_of(r * step, step), step)

        def score(s, k):
            row = s * (TILE // LANES) + k
            return m_ref[s][here, k * LANES : (k + 1) * LANES] + c_ref[row : row + 1, :]

        each = [(s, k) for s in range(slabs) for k in range(TILE // LANES)]
        top = functools.reduce(jnp.maximum, [score(s, k) for s, k in each])
        top = jnp.broadcast_to(jnp.max(top, axis=1, keepdims=True), top.shape)
        acc_ref[here, :] = functools.reduce(jnp.add, [jnp.exp2(score(s, k) - top) for s, k in each])
        top_ref[here, :] = top
        return carry

    lax.fori_loop(0, rows // step, body, 0)


def fast_rows(m_ref, v_ref, acc_ref):
    slabs, rows = len(m_ref), m_ref[0].shape[0]
    step = 256

    def body(r, carry):
        here = pl.ds(pl.multiple_of(r * step, step), step)
        total = None
        for s in range(slabs):
            for k in range(TILE // LANES):
                row = s * (TILE // LANES) + k
                term = m_ref[s][here, k * LANES : (k + 1) * LANES] * v_ref[row : row + 1, :]
                total = term if total is None else total + term
        acc_ref[here, :] = total
        return carry

    lax.fori_loop(0, rows // step, body, 0, unroll=2)


def finish_rows(fast, shift, acc_ref, top_ref, bits_ref, row_ref, out_ref):
    gather_rows(acc_ref, row_ref)

    @pl.when(fast)
    def _():
        bits_ref[...] = jnp.broadcast_to(shift, bits_ref.shape)

    @pl.when(jnp.logical_not(fast))
    def _():
        first_rows(top_ref, bits_ref)

    out_ref[...] = jnp.broadcast_to((log2(row_ref[...]) + bits_ref[...])[None], out_ref.shape)


def cells_kernel(y_ref, ynorm_ref):
    norms(y_ref, ynorm_ref)


def first_kernel(x_ref, y_ref, ynorm_ref, m_ref, bound_ref, xnorm_ref, out_ref, v_ref, acc_ref, top_ref, bits_ref, row_ref):
    rows, depth = x_ref.shape
    slabs = len(m_ref)
    scale = 2.0 * LOG2E / (EPS * depth)
    norms(x_ref, xnorm_ref)
    most_x = jnp.max(xnorm_ref[...], keepdims=True)
    most_y = jnp.max(ynorm_ref[...], keepdims=True)
    bound = scale * jnp.sqrt(most_x * most_y)
    bound_ref[...] = jnp.broadcast_to(bound, bound_ref.shape)
    fast = jnp.max(bound) <= LIMIT
    c_bits = ynorm_ref[...] * (-LOG2E / (EPS * depth))
    top_c = jnp.max(c_bits, keepdims=True)

    step = min(512, rows)

    def scores(s, here):
        ys = y_ref[s * TILE : (s + 1) * TILE, :]
        return lax.dot_general(x_ref[here, :], ys, NT, preferred_element_type=F32) * scale

    @pl.when(fast)
    def _():
        v_ref[...] = jnp.exp2(c_bits - top_c + SHIFT)
        for s in range(slabs):
            for r in range(rows // step):
                here = slice(r * step, (r + 1) * step)
                power = jnp.exp2(scores(s, here))
                m_ref[s][here, :] = power
                total = None if s == 0 else acc_ref[here, :]
                for k in range(TILE // LANES):
                    row = s * (TILE // LANES) + k
                    term = power[:, k * LANES : (k + 1) * LANES] * v_ref[row : row + 1, :]
                    total = term if total is None else total + term
                acc_ref[here, :] = total

    @pl.when(jnp.logical_not(fast))
    def _():
        v_ref[...] = c_bits

        for s in range(slabs):
            m_ref[s][...] = scores(s, slice(None))
        careful_rows(m_ref, v_ref, acc_ref, top_ref)

    finish_rows(fast, top_c - SHIFT, acc_ref, top_ref, bits_ref, row_ref, out_ref)


def row_kernel(log_ends, m_ref, bound_ref, got_ref, out_ref, v_ref, acc_ref, top_ref, bits_ref, row_ref):
    fast = fast_of(bound_ref)
    c_bits = log_ends - combine(got_ref[...])
    top_c = jnp.max(c_bits, keepdims=True)

    @pl.when(fast)
    def _():
        v_ref[...] = jnp.exp2(c_bits - top_c + SHIFT)
        fast_rows(m_ref, v_ref, acc_ref)

    @pl.when(jnp.logical_not(fast))
    def _():
        v_ref[...] = c_bits
        careful_rows(m_ref, v_ref, acc_ref, top_ref)

    finish_rows(fast, top_c - SHIFT, acc_ref, top_ref, bits_ref, row_ref, out_ref)


def col_kernel(log_cells, m_ref, bound_ref, got_ref, out_ref, u_ref, sum_ref):
    slabs, rows = len(m_ref), m_ref[0].shape[0]
    fast = fast_of(bound_ref)
    f_bits = log_cells - combine(got_ref[...])
    top_f = jnp.max(f_bits, keepdims=True)
    step = 64

    @pl.when(fast)
    def _():
        spread(jnp.exp2(f_bits - top_f + SHIFT), u_ref)
        wide = 8 if slabs % 8 == 0 else 1
        for s in range(0, slabs, wide):

            def body(r, totals):
                here = pl.ds(pl.multiple_of(r * step, step), step)
                u = u_ref[here, :]
                new = []
                for w in range(wide):
                    for k in range(TILE // LANES):
                        term = m_ref[s + w][here, k * LANES : (k + 1) * LANES] * u
                        total = totals[len(new)]
                        for g in range(step // 8):
                            total = total + term[g * 8 : (g + 1) * 8, :]
                        new.append(total)
                return tuple(new)

            n = wide * (TILE // LANES)
            totals = lax.fori_loop(0, rows // step, body, (jnp.zeros((8, LANES), F32),) * n, unroll=2)
            for k in range(n):
                row = s * (TILE // LANES) + k
                sum_ref[row : row + 1, :] = jnp.sum(totals[k], axis=0, keepdims=True)
        sum_ref[...] = log2(sum_ref[...]) + (top_f - SHIFT)

    @pl.when(jnp.logical_not(fast))
    def _():
        spread(f_bits, u_ref)
        for s in range(slabs):
            for k in range(TILE // LANES):

                def score(r):
                    here = pl.ds(pl.multiple_of(r * step, step), step)
                    return m_ref[s][here, k * LANES : (k + 1) * LANES] + u_ref[here, :]

                def most(r, top):
                    return jnp.maximum(top, score(r))

                top = lax.fori_loop(0, rows // step, most, jnp.full((step, LANES), -3.0e38, F32))
                top = jnp.max(top, axis=0, keepdims=True)

                def add(r, total):
                    return total + jnp.exp2(score(r) - top)

                total = lax.fori_loop(0, rows // step, add, jnp.zeros((step, LANES), F32))
                row = s * (TILE // LANES) + k
                sum_ref[row : row + 1, :] = log2(jnp.sum(total, axis=0, keepdims=True)) + top

    out_ref[...] = jnp.broadcast_to(sum_ref[...][None], out_ref.shape)


def last_kernel(log_cells, log_ends, m_ref, bound_ref, rows_ref, cols_ref, y_ref, xnorm_ref, ynorm_ref,
                end_ref, cell_ref, out_ref, u_ref, v_ref, mass_ref, row_ref):
    slabs, rows = len(m_ref), m_ref[0].shape[0]
    depth = y_ref.shape[1]
    fast = fast_of(bound_ref)
    f_bits = log_cells - combine(rows_ref[...])
    c_bits = log_ends - combine(cols_ref[...])
    end_ref[...] = f_bits * (EPS / LOG2E) + xnorm_ref[...] * (1.0 / depth)
    cell_ref[...] = c_bits * (EPS / LOG2E) + ynorm_ref[...] * (1.0 / depth)
    top_f = jnp.max(f_bits, keepdims=True) - 24.0
    step = min(1024, rows)

    def weigh(weight):
        def body(r, carry):
            here = pl.ds(pl.multiple_of(r * step, step), step)
            u = u_ref[here, :]
            moved = None
            mass = None
            for s in range(slabs):
                parts = []
                for k in range(TILE // LANES):
                    row = s * (TILE // LANES) + k
                    part = weight(m_ref[s][here, k * LANES : (k + 1) * LANES], u, v_ref[row : row + 1, :])
                    mass = part if mass is None else mass + part
                    parts.append(part.astype(BF16))
                term = jnp.dot(
                    jnp.concatenate(parts, axis=1), y_ref[s * TILE : (s + 1) * TILE, :], preferred_element_type=F32
                )
                moved = term if moved is None else moved + term
            mass_ref[here, :] = mass
            for g in range(step // LANES):
                block = moved[g * LANES : (g + 1) * LANES, :].astype(BF16)
                for half in range(depth // LANES):
                    here = slice(half * LANES, (half + 1) * LANES)
                    out_ref[r * (step // LANES) + g, here, :] = block[:, here]
            return carry

        lax.fori_loop(0, rows // step, body, 0)

    @pl.when(fast)
    def _():
        spread(jnp.exp2(f_bits - top_f), u_ref)
        v_ref[...] = jnp.exp2(c_bits + (top_f - log_cells))
        weigh(lambda m, u, v: (m * u) * v)

    @pl.when(jnp.logical_not(fast))
    def _():
        spread(f_bits, u_ref)
        v_ref[...] = c_bits - log_cells
        weigh(lambda m, u, v: jnp.exp2((m + u) + v))

    gather_rows(mass_ref, row_ref)
    for b in range(rows // LANES):
        mass = jnp.broadcast_to(row_ref[b : b + 1, :], (16, LANES))
        high = mass.astype(BF16).astype(F32)
        mid = (mass - high).astype(BF16).astype(F32)
        low = mass - high - mid
        place = lax.broadcasted_iota(jnp.int32, mass.shape, 0)
        split = jnp.where(place < 4, high, jnp.where(place < 8, mid, low))
        out_ref[b, depth : depth + 16, :] = split.astype(BF16)


def end_kernel(got_ref, x_ref, out_ref):
    count, size, _ = got_ref.shape
    depth = size - 16
    split = functools.reduce(jnp.add, [got_ref[n, depth:size, :].astype(F32) for n in range(count)])
    mass = (split[0:1, :] + split[4:5, :]) + split[8:9, :]
    wide = jnp.broadcast_to(mass, (LANES, LANES)).T
    for half in range(depth // LANES):
        here = slice(half * LANES, (half + 1) * LANES)
        moved = functools.reduce(jnp.add, [got_ref[n, here, :].astype(F32) for n in range(count)])
        out_ref[:, here] = x_ref[:, here].astype(F32) * wide - moved


def call(kernel, outs, scratch, limit_mib=16, cost=None):
    return pl.pallas_call(
        kernel,
        name=getattr(kernel, "func", kernel).__name__,
        out_shape=outs,
        cost_estimate=cost,
        scratch_shapes=[pltpu.VMEM(s, F32) if isinstance(s, tuple) else s for s in scratch],
        compiler_params=pltpu.CompilerParams(vmem_limit_bytes=limit_mib << 20),
    )


def swap(parts, axis):
    return lax.all_to_all(parts, axis, 0, 0, tiled=True)


def grouped(kernel, at, count):
    def body(*refs):
        kernel(*refs[:at], refs[at : at + count], *refs[at + count :])

    body.__name__ = getattr(kernel, "func", kernel).__name__
    return body


def pin(m):
    return pltpu.with_memory_space_constraint(m, pltpu.VMEM)


def shards(endpoints, cells):
    n_row, n_col = lax.axis_size("row"), lax.axis_size("col")
    own, depth = endpoints.shape
    rows, cols = own * n_col, cells.shape[0]
    log_cells = math.log2(cols * n_col)
    log_ends = math.log2(rows * n_row)
    rb, cb = rows // LANES, cols // LANES
    block_x = swap(jnp.broadcast_to(endpoints[None], (n_col, own, depth)), "col").reshape(rows, depth)

    arr = lambda *shape: pltpu.VMEM(shape, F32)
    hbm = lambda *shape: jax.ShapeDtypeStruct(shape, F32)
    row_scratch = [(cb, LANES), (rows, LANES), (rows, LANES), (rb, LANES), (rb, LANES)]
    col_scratch = [(rows, LANES), (cb, LANES)]
    cost = pl.CostEstimate(flops=cols * depth * 64, bytes_accessed=4 * cols * depth, transcendentals=0)
    ynorm = call(cells_kernel, arr(cb, LANES), [], cost=cost)(pin(cells))
    ynorm = lax.ppermute(ynorm, "row", [(n, n ^ 1) for n in range(n_row)])
    slabs = cols // TILE
    *m, bound, xnorm, sums = call(
        grouped(first_kernel, 3, slabs),
        [pltpu.VMEM((rows, TILE), F32)] * slabs + [arr(8, LANES), arr(rb, LANES), arr(n_col, rb, LANES)],
        row_scratch,
    )(pin(block_x), pin(cells), pin(ynorm))
    for step in range(ITERS):
        if step > 0:
            sums = call(grouped(functools.partial(row_kernel, log_ends), 0, slabs), arr(n_col, rb, LANES), row_scratch)(*map(pin, m), pin(bound), pin(got_cols))
        got_rows = swap(sums, "col")
        sums = call(grouped(functools.partial(col_kernel, log_cells), 0, slabs), arr(n_row, cb, LANES), col_scratch)(*map(pin, m), pin(bound), pin(got_rows))
        got_cols = swap(sums, "row")
    end_pot, cell_pot, moved = call(
        grouped(functools.partial(last_kernel, log_cells, log_ends), 0, slabs),
        [hbm(rb, LANES), hbm(cb, LANES), pltpu.VMEM((n_col, depth + 16, own), BF16)],
        [(rows, LANES), (cb, LANES), (rows, LANES), (rb, LANES)],
    )(*map(pin, m), pin(bound), pin(got_rows), pin(got_cols), pin(cells), pin(xnorm), pin(ynorm))
    displacement = call(end_kernel, hbm(own, depth), [])(pin(swap(moved, "col")), endpoints)
    return end_pot.reshape(rows), cell_pot.reshape(cols), displacement


def solution(mesh):
    return jax.shard_map(
        shards,
        mesh=mesh,
        in_specs=(P(("row", "col"), None), P("col", None)),
        out_specs=(P("row"), P("col"), P(("row", "col"), None)),
        check_vma=False,
    )
```

```python
import functools
import math

import jax
import jax.numpy as jnp
from jax import lax
from jax.experimental import pallas as pl
from jax.experimental.pallas import tpu as pltpu
from jax.sharding import PartitionSpec as P

ITERS = 3
EPS = 0.1
LOG2E = math.log2(math.e)
LIMIT = 52.0
SHIFT = 50.0
LANES = 128
TILE = 512
F32 = jnp.float32
BF16 = jnp.bfloat16
NT = (((1,), (1,)), ((), ()))


def log2(x):
    return jnp.log(x) * LOG2E


def combine(parts):
    top = jnp.max(parts, axis=0)
    return top + log2(jnp.sum(jnp.exp2(parts - top[None]), axis=0))


def norms(src_ref, out_ref):
    rows, depth = src_ref.shape
    step = min(TILE, rows)
    ones = jnp.ones((8, depth), BF16)
    for t in range(rows // step):
        val = src_ref[t * step : (t + 1) * step, :].astype(F32)
        sq = val * val
        high = sq.astype(BF16)
        low = (sq - high.astype(F32)).astype(BF16)
        got = lax.dot_general(ones, high, NT, preferred_element_type=F32)
        got = got + lax.dot_general(ones, low, NT, preferred_element_type=F32)
        for k in range(step // LANES):
            row = t * (step // LANES) + k
            out_ref[row : row + 1, :] = got[0:1, k * LANES : (k + 1) * LANES]


def holder(b, nx, ny):
    g, d = divmod(b, nx)
    turned = d * ny + g if nx == ny else b
    odd = lax.rem(lax.axis_index("row"), 2) == 1
    return lax.axis_index("col") ^ jnp.where(odd, turned, b)


def spread(row, out_ref, at):
    out_ref[at : at + LANES, :] = jnp.broadcast_to(row, (LANES, LANES)).T


def lane_sums(block):
    return jnp.sum(block.T, axis=0, keepdims=True)


def is_fast(bound_ref):
    return jnp.max(bound_ref[0:1, :]) <= LIMIT


def all_fast(bounds):
    return jnp.max(functools.reduce(jnp.maximum, [b[0:1, :] for b in bounds])) <= LIMIT


def score_of(fast, m):
    return jnp.where(fast, log2(m), m)


def careful_rows(slabs, c_ref, acc_ref, top_ref, at):
    step = 8

    def body(r, carry):
        here = pl.ds(pl.multiple_of(r * step, step), step)
        there = pl.ds(pl.multiple_of(at + r * step, step), step)

        def score(s, k):
            row = s * (TILE // LANES) + k
            return slabs[s][here, k * LANES : (k + 1) * LANES] + c_ref[row : row + 1, :]

        each = [(s, k) for s in range(len(slabs)) for k in range(TILE // LANES)]
        top = functools.reduce(jnp.maximum, [score(s, k) for s, k in each])
        top = jnp.broadcast_to(jnp.max(top, axis=1, keepdims=True), top.shape)
        acc_ref[there, :] = functools.reduce(jnp.add, [jnp.exp2(score(s, k) - top) for s, k in each])
        top_ref[there, :] = top
        return carry

    lax.fori_loop(0, slabs[0].shape[0] // step, body, 0)


def fast_rows(slabs, v_ref, acc_ref, at, step=128):

    def body(r, carry):
        here = pl.ds(pl.multiple_of(r * step, step), step)
        total = None
        for s in range(len(slabs)):
            for k in range(TILE // LANES):
                row = s * (TILE // LANES) + k
                term = slabs[s][here, k * LANES : (k + 1) * LANES] * v_ref[row : row + 1, :]
                total = term if total is None else total + term
        acc_ref[pl.ds(pl.multiple_of(at + r * step, step), step), :] = total
        return carry

    lax.fori_loop(0, slabs[0].shape[0] // step, body, 0)


def cells_kernel(y_ref, ynorm_ref):
    norms(y_ref, ynorm_ref)


def join_kernel(ynorm_ref, got_refs, out_ref, start_ref):
    for d, got_ref in enumerate(got_refs):
        out_ref[d * LANES : (d + 1) * LANES, :] = got_ref[...]
    start_ref[...] = ynorm_ref[0 : start_ref.shape[0], :]


def first_kernel(g, x_ref, y_ref, ynorm_ref, before_ref, m_ref, bound_ref, xnorm_ref, out_ref,
                 v_ref, acc_ref, top_ref, row_ref):
    rows, depth = x_ref.shape
    blocks = rows // LANES
    slabs = len(m_ref)
    scale = 2.0 * LOG2E / (EPS * depth)
    norms(x_ref, xnorm_ref)
    most_x = jnp.max(xnorm_ref[0:blocks, :], keepdims=True)
    most_y = jnp.max(ynorm_ref[...], keepdims=True)
    bound = scale * jnp.sqrt(most_x * most_y)
    bound_ref[...] = jnp.broadcast_to(bound, bound_ref.shape)
    fast = jnp.max(bound) <= LIMIT
    c_bits = ynorm_ref[...] * (-LOG2E / (EPS * depth))
    top_c = jnp.max(c_bits, keepdims=True)

    def scores(s, here=slice(None)):
        ys = y_ref[s * TILE : (s + 1) * TILE, :]
        return lax.dot_general(x_ref[here, :], ys, NT, preferred_element_type=F32) * scale

    @pl.when(fast)
    def _():
        v_ref[...] = jnp.exp2(c_bits - top_c + SHIFT)
        for s in range(slabs):
            power = jnp.exp2(scores(s))
            m_ref[s][...] = power
            total = None if s == 0 else acc_ref[...]
            for k in range(TILE // LANES):
                row = s * (TILE // LANES) + k
                term = power[:, k * LANES : (k + 1) * LANES] * v_ref[row : row + 1, :]
                total = term if total is None else total + term
            acc_ref[...] = total
        top_ref[...] = jnp.broadcast_to(top_c - SHIFT, top_ref.shape)

    @pl.when(jnp.logical_not(fast))
    def _():
        v_ref[...] = c_bits

        def piece(r, carry):
            here = pl.ds(pl.multiple_of(r * 64, 64), 64)
            for s in range(slabs):
                m_ref[s][here, :] = scores(s, here)
            return carry

        lax.fori_loop(0, rows // 64, piece, 0)
        careful_rows(m_ref, v_ref, acc_ref, top_ref, 0)

    row_ref[...] = before_ref[...]
    for d in range(blocks):
        here = slice(d * LANES, (d + 1) * LANES)
        total = log2(lane_sums(acc_ref[here, :])) + top_ref[here, :].T[0:1, :]
        row_ref[pl.ds(holder(g * blocks + d, blocks, before_ref.shape[0] // blocks), 1), :] = total
    out_ref[...] = row_ref[...] if out_ref.ndim == 2 else jnp.broadcast_to(row_ref[...][None], out_ref.shape)


def row_kernel(log_ends, m_ref, bounds, got_ref, out_ref, v_ref, c_ref, acc_ref, top_ref, row_ref):
    slabs = len(m_ref) // len(bounds)
    rows = m_ref[0].shape[0]
    blocks = rows // LANES
    c_ref[...] = log_ends - combine(got_ref[...])
    top_c = jnp.max(c_ref[...], keepdims=True)
    v_ref[...] = jnp.exp2(c_ref[...] - top_c + SHIFT)
    quick = all_fast(bounds)

    def finish(g, at, shift):
        for d in range(blocks):
            here = slice(at + d * LANES, at + (d + 1) * LANES)
            place = pl.ds(holder(g * blocks + d, blocks, len(bounds)), 1)
            row_ref[place, :] = log2(lane_sums(acc_ref[here, :])) + shift(here)

    @pl.when(quick)
    def _():
        for g in range(len(bounds)):
            fast_rows(m_ref[g * slabs : (g + 1) * slabs], v_ref, acc_ref, g * rows)
        for b in range(len(bounds) * blocks):
            row_ref[pl.ds(holder(b, blocks, len(bounds)), 1), :] = lane_sums(acc_ref[b * LANES : (b + 1) * LANES, :])
        row_ref[...] = log2(row_ref[...]) + (top_c - SHIFT)

    for g in range(len(bounds)):
        fast = is_fast(bounds[g])
        part = m_ref[g * slabs : (g + 1) * slabs]

        @pl.when(jnp.logical_not(quick) & fast)
        def _():
            fast_rows(part, v_ref, acc_ref, 0, 16)
            finish(g, 0, lambda here: top_c - SHIFT)

        @pl.when(jnp.logical_not(fast))
        def _():
            careful_rows(part, c_ref, acc_ref, top_ref, 0)
            finish(g, 0, lambda here: top_ref[here, :].T[0:1, :])

    out_ref[...] = jnp.broadcast_to(row_ref[...][None], out_ref.shape)


def col_kernel(log_cells, m_ref, bounds, got_ref, out_ref, u_ref, f_ref, sum_ref):
    slabs = len(m_ref) // len(bounds)
    rows = m_ref[0].shape[0]
    fast = all_fast(bounds)
    f_bits = log_cells - combine(got_ref[...])
    top_f = jnp.max(f_bits, keepdims=True)
    step = 64
    n = slabs * (TILE // LANES)

    def place():
        for b in range(rows * len(bounds) // LANES):
            spread(f_ref[pl.ds(holder(b, rows // LANES, len(bounds)), 1), :], u_ref, b * LANES)

    @pl.when(fast)
    def _():
        f_ref[...] = jnp.exp2(f_bits - top_f + SHIFT)
        place()
        totals = (jnp.zeros((8, LANES), F32),) * n
        for g in range(len(bounds)):

            def body(r, totals):
                here = pl.ds(pl.multiple_of(r * step, step), step)
                u = u_ref[pl.ds(pl.multiple_of(g * rows + r * step, step), step), :]
                new = []
                for s in range(slabs):
                    for k in range(TILE // LANES):
                        term = m_ref[g * slabs + s][here, k * LANES : (k + 1) * LANES] * u
                        total = totals[len(new)]
                        for part in range(step // 8):
                            total = total + term[part * 8 : (part + 1) * 8, :]
                        new.append(total)
                return tuple(new)

            totals = lax.fori_loop(0, rows // step, body, totals)
        for k in range(n):
            sum_ref[k : k + 1, :] = jnp.sum(totals[k], axis=0, keepdims=True)
        sum_ref[...] = log2(sum_ref[...]) + (top_f - SHIFT)

    @pl.when(jnp.logical_not(fast))
    def _():
        f_ref[...] = f_bits
        place()
        step = 8
        for s in range(slabs):

            def score(g, r):
                here = pl.ds(pl.multiple_of(r * step, step), step)
                u = u_ref[pl.ds(pl.multiple_of(g * rows + r * step, step), step), :]
                u = jnp.concatenate([u] * (TILE // LANES), axis=1)
                return score_of(is_fast(bounds[g]), m_ref[g * slabs + s][here, :]) + u

            def add(g, r, carry):
                top, total = carry
                new = score(g, r)
                most = jnp.maximum(top, new)
                return most, total * jnp.exp2(top - most) + jnp.exp2(new - most)

            carry = jnp.full((step, TILE), -3.0e38, F32), jnp.zeros((step, TILE), F32)
            for g in range(len(bounds)):
                carry = lax.fori_loop(0, rows // step, functools.partial(add, g), carry)
            tops, total = carry
            top = jnp.max(tops, axis=0, keepdims=True)
            total = jnp.sum(total * jnp.exp2(tops - top), axis=0, keepdims=True)
            total = log2(total) + top
            for k in range(TILE // LANES):
                row = s * (TILE // LANES) + k
                sum_ref[row : row + 1, :] = total[:, k * LANES : (k + 1) * LANES]

    out_ref[...] = jnp.broadcast_to(sum_ref[...][None], out_ref.shape)


def last_kernel(g, log_cells, log_ends, m_ref, bounds, xnorms, rows_ref, cols_ref, y_ref, ynorm_ref, before_ref,
                out_ref, after_ref, *rest):
    *pots, f_ref, u_ref, v_ref, mass_ref, row_ref = rest
    slabs = len(m_ref)
    rows, depth = m_ref[0].shape[0], y_ref.shape[1]
    blocks = rows // LANES
    fast = is_fast(bounds[g])
    f_bits = log_cells - combine(rows_ref[...])
    c_bits = log_ends - combine(cols_ref[...])
    f_ref[...] = f_bits
    mine = [f_ref[pl.ds(holder(g * blocks + d, blocks, len(bounds)), 1), :] for d in range(blocks)]
    top_f = jnp.max(functools.reduce(jnp.maximum, mine), keepdims=True) - 24.0

    def weigh(here, weight):
        u = u_ref[here, :]
        moved = None
        mass = None
        for s in range(slabs):
            parts = []
            for k in range(TILE // LANES):
                row = s * (TILE // LANES) + k
                part = weight(m_ref[s][here, k * LANES : (k + 1) * LANES], u, v_ref[row : row + 1, :])
                mass = part if mass is None else mass + part
                parts.append(part.astype(BF16))
            term = jnp.dot(jnp.concatenate(parts, axis=1), y_ref[s * TILE : (s + 1) * TILE, :], preferred_element_type=F32)
            moved = term if moved is None else moved + term
        mass_ref[here, :] = mass
        out_ref[here, :] = moved.astype(out_ref.dtype)

    @pl.when(fast)
    def _():
        v_ref[...] = jnp.exp2(c_bits + (top_f - log_cells))
        for d in range(blocks):
            spread(jnp.exp2(mine[d] - top_f), u_ref, d * LANES)
        weigh(slice(0, rows), lambda m, u, v: (m * u) * v)

    @pl.when(jnp.logical_not(fast))
    def _():
        v_ref[...] = c_bits - log_cells
        for d in range(blocks):
            spread(mine[d], u_ref, d * LANES)
        step = 16

        def body(r, carry):
            here = pl.ds(pl.multiple_of(r * step, step), step)
            weigh(here, lambda m, u, v: jnp.exp2((m + u) + v))
            return carry

        lax.fori_loop(0, rows // step, body, 0)

    row_ref[...] = jnp.zeros_like(row_ref)
    for d in range(blocks):
        row_ref[d : d + 1, :] = lane_sums(mass_ref[d * LANES : (d + 1) * LANES, :])
    mass = row_ref[...]
    if out_ref.dtype == F32:
        out_ref[rows : rows + 8, :] = jnp.concatenate([mass, mass], axis=1)
    else:
        high = mass.astype(BF16).astype(F32)
        mid = (mass - high).astype(BF16).astype(F32)
        low = mass - high - mid
        first = jnp.concatenate([high, mid], axis=1)
        second = jnp.concatenate([low, low], axis=1)
        out_ref[rows : rows + 16, :] = jnp.concatenate([first, second], axis=0).astype(BF16)
    after_ref[...] = before_ref[...]
    if pots:
        end_ref, cell_ref = pots
        for p, xnorm_ref in enumerate(xnorms):
            for d in range(blocks):
                f_ref[pl.ds(holder(p * blocks + d, blocks, len(bounds)), 1), :] = xnorm_ref[d : d + 1, :]
        end_ref[...] = f_bits * (EPS / LOG2E) + f_ref[...] * (1.0 / depth)
        cell_ref[...] = c_bits * (EPS / LOG2E) + ynorm_ref[...] * (1.0 / depth)


def sum_kernel(own_ref, got_refs, out_refs):
    rows = own_ref.shape[0] - 8
    mass = own_ref[rows : rows + 8, :LANES]
    for got_ref in got_refs:
        parts = got_ref[rows : rows + 16, :].astype(F32)
        mass = mass + ((parts[0:8, :LANES] + parts[0:8, LANES:]) + parts[8:16, :LANES])
    wide = jnp.concatenate([mass, mass], axis=1)
    for d, out_ref in enumerate(out_refs):
        here = slice(d * LANES, (d + 1) * LANES)
        total = own_ref[here, :]
        for got_ref in got_refs:
            total = total + got_ref[here, :].astype(F32)
        out_ref[0:LANES, :] = total
        out_ref[LANES : LANES + 8, :] = jnp.broadcast_to(wide[d : d + 1, :], (8, wide.shape[1]))


def end_kernel(x_ref, got_refs, out_ref):
    total = functools.reduce(jnp.add, [got_ref[...] for got_ref in got_refs])
    wide = jnp.broadcast_to(total[LANES : LANES + 1, :LANES], (LANES, LANES)).T
    x = x_ref[...].astype(F32)
    out_ref[:, :LANES] = x[:, :LANES] * wide - total[:LANES, :LANES]
    out_ref[:, LANES:] = x[:, LANES:] * wide - total[:LANES, LANES:]


def grouped(kernel, at, *counts):
    def body(*refs):
        groups, n = [], at
        for count in counts:
            groups.append(refs[n : n + count] if count else refs[n])
            n += max(count, 1)
        kernel(*refs[:at], *groups, *refs[n:])

    body.__name__ = getattr(kernel, "func", kernel).__name__
    return body


def call(kernel, outs, scratch, limit_mib=16, cost=None):
    return pl.pallas_call(
        kernel,
        name=getattr(kernel, "func", kernel).__name__,
        out_shape=outs,
        cost_estimate=cost,
        scratch_shapes=[pltpu.VMEM(s, F32) for s in scratch],
        compiler_params=pltpu.CompilerParams(vmem_limit_bytes=limit_mib << 20),
    )


def swap(parts, axis):
    return lax.all_to_all(parts, axis, 0, 0, tiled=True)


def flip(value, by, turned):
    n_row, n_col = lax.axis_size("row"), lax.axis_size("col")
    pairs = [(r * n_col + n, r * n_col + (n ^ (turned if r % 2 else by))) for r in range(n_row) for n in range(n_col)]
    return lax.ppermute(value, ("row", "col"), pairs)


def pin(m):
    return pltpu.with_memory_space_constraint(m, pltpu.VMEM)


def inside(*shape, dtype=F32):
    return pltpu.VMEM(shape, dtype)


def shards(endpoints, cells):
    n_row, n_col = lax.axis_size("row"), lax.axis_size("col")
    nx = 1 << ((n_col.bit_length() - 1) // 2)
    ny = n_col // nx
    square = nx == ny

    def between(value, d):
        return flip(value, d, d * ny if square else d)

    def across(value, g):
        return flip(value, g * nx, g if square else g * nx)

    own, depth = endpoints.shape
    rows, cols, part = own * n_col, cells.shape[0], own * nx
    log_cells = math.log2(cols * n_col)
    log_ends = math.log2(rows * n_row)
    rb, cb, slabs = rows // LANES, cols // LANES, cols // TILE
    order = sorted(range(1, ny), key=lambda g: min(g, ny - g))
    work = 2 * part * cols * depth
    small = pl.CostEstimate(flops=work // 16, bytes_accessed=part * cols // 4, transcendentals=0)
    cost = pl.CostEstimate(flops=work, bytes_accessed=4 * part * cols, transcendentals=0)

    ynorm = call(cells_kernel, inside(cb, LANES), [], cost=cost)(pin(cells))
    near, sums = call(
        grouped(join_kernel, 1, nx),
        [inside(part, depth, dtype=BF16), inside(rb, LANES)],
        [],
    )(pin(ynorm), *[pin(between(endpoints, d)) if d else endpoints for d in range(nx)])
    x = [near] + [across(near, g) for g in range(1, ny)]

    m, bounds, xnorms = [None] * ny, [None] * ny, [None] * ny
    for g in [0] + order:
        out = inside(n_col, rb, LANES) if g == order[-1] else inside(rb, LANES)
        *m[g], bounds[g], xnorms[g], sums = call(
            grouped(functools.partial(first_kernel, g), 4, slabs),
            [inside(part, TILE)] * slabs + [inside(8, LANES), inside(8, LANES), out],
            [(cb, LANES), (part, LANES), (part, LANES), (rb, LANES)],
            cost=cost,
        )(pin(x[g]), pin(cells), pin(ynorm), pin(sums))
    block = [pin(slab) for g in range(ny) for slab in m[g]]
    flags = [pin(bound) for bound in bounds]

    for step in range(ITERS):
        if step > 0:
            sums = call(
                grouped(functools.partial(row_kernel, log_ends), 0, ny * slabs, ny),
                inside(n_col, rb, LANES),
                [(cb, LANES), (cb, LANES), (rows, LANES), (part, LANES), (rb, LANES)],
            )(*block, *flags, pin(got_cols))
        got_rows = swap(sums, "col")
        sums = call(
            grouped(functools.partial(col_kernel, log_cells), 0, ny * slabs, ny),
            inside(n_row, cb, LANES),
            [(rows, LANES), (rb, LANES), (cb, LANES)],
        )(*block, *flags, pin(got_rows))
        got_cols = swap(sums, "row")

    token = inside(8, LANES)
    sent, after = [], bounds[0]
    for g in order[::-1] + [0]:
        message = inside(part + 16, depth, dtype=BF16) if g else inside(part + 8, depth)
        pots = [] if g else [jax.ShapeDtypeStruct((rb, LANES), F32), jax.ShapeDtypeStruct((cb, LANES), F32)]
        message, after, *pots = call(
            grouped(functools.partial(last_kernel, g, log_cells, log_ends), 0, slabs, ny, ny),
            [message, token] + pots,
            [(rb, LANES), (part, LANES), (cb, LANES), (part, LANES), (8, LANES)],
            cost=small,
        )(*map(pin, m[g]), *flags, *map(pin, xnorms), pin(got_rows), pin(got_cols), pin(cells), pin(ynorm), pin(after))
        sent.append(across(message, g) if g else message)
    end_pot, cell_pot = pots
    sums = call(
        grouped(sum_kernel, 0, 0, ny - 1, nx),
        [inside(own + 8, depth)] * nx,
        [],
    )(pin(sent[-1]), *map(pin, sent[:-1]))
    sums = [sums[0]] + [between(sums[d], d) for d in range(1, nx)]
    displacement = call(
        grouped(end_kernel, 1, nx),
        jax.ShapeDtypeStruct((own, depth), F32),
        [],
    )(endpoints, *map(pin, sums))
    return end_pot.reshape(rows), cell_pot.reshape(cols), displacement


def solution(mesh):
    return jax.shard_map(
        shards,
        mesh=mesh,
        in_specs=(P(("row", "col"), None), P("col", None)),
        out_specs=(P("row"), P("col"), P(("row", "col"), None)),
        check_vma=False,
    )
```

```python
import functools
import math

import jax
import jax.numpy as jnp
from jax import lax
from jax.experimental import pallas as pl
from jax.experimental.pallas import tpu as pltpu
from jax.sharding import PartitionSpec as P

ITERS = 3
EPS = 0.1
LOG2E = math.log2(math.e)
LIMIT = 52.0
SHIFT = 50.0
LANES = 128
TILE = 512
F32 = jnp.float32
BF16 = jnp.bfloat16
NT = (((1,), (1,)), ((), ()))


def log2(x):
    return jnp.log(x) * LOG2E


def combine(parts):
    top = jnp.max(parts, axis=0)
    return top + log2(jnp.sum(jnp.exp2(parts - top[None]), axis=0))


def norms(src_ref, out_ref):
    rows, depth = src_ref.shape
    step = min(TILE, rows)
    ones = jnp.ones((8, depth), BF16)
    for t in range(rows // step):
        val = src_ref[t * step : (t + 1) * step, :].astype(F32)
        sq = val * val
        high = sq.astype(BF16)
        low = (sq - high.astype(F32)).astype(BF16)
        got = lax.dot_general(ones, high, NT, preferred_element_type=F32)
        got = got + lax.dot_general(ones, low, NT, preferred_element_type=F32)
        for k in range(step // LANES):
            row = t * (step // LANES) + k
            out_ref[row : row + 1, :] = got[0:1, k * LANES : (k + 1) * LANES]


def holder(b, nx, ny):
    g, d = divmod(b, nx)
    turned = d * ny + g if nx == ny else b
    odd = lax.rem(lax.axis_index("row"), 2) == 1
    return lax.axis_index("col") ^ jnp.where(odd, turned, b)


def spread(row, out_ref, at):
    out_ref[at : at + LANES, :] = jnp.broadcast_to(row, (LANES, LANES)).T


def lane_sums(block):
    return jnp.sum(block.T, axis=0, keepdims=True)


def is_fast(bound_ref):
    return jnp.max(bound_ref[0:1, :]) <= LIMIT


def all_fast(bounds):
    return jnp.max(functools.reduce(jnp.maximum, [b[0:1, :] for b in bounds])) <= LIMIT


def score_of(fast, m):
    return jnp.where(fast, log2(m), m)


def careful_rows(slabs, c_ref, acc_ref, top_ref, at):
    step = 8

    def body(r, carry):
        here = pl.ds(pl.multiple_of(r * step, step), step)
        there = pl.ds(pl.multiple_of(at + r * step, step), step)

        def score(s, k):
            row = s * (TILE // LANES) + k
            return slabs[s][here, k * LANES : (k + 1) * LANES] + c_ref[row : row + 1, :]

        each = [(s, k) for s in range(len(slabs)) for k in range(TILE // LANES)]
        top = functools.reduce(jnp.maximum, [score(s, k) for s, k in each])
        top = jnp.broadcast_to(jnp.max(top, axis=1, keepdims=True), top.shape)
        acc_ref[there, :] = functools.reduce(jnp.add, [jnp.exp2(score(s, k) - top) for s, k in each])
        top_ref[there, :] = top
        return carry

    lax.fori_loop(0, slabs[0].shape[0] // step, body, 0)


def fast_rows(slabs, v_ref, acc_ref, at, step=256):

    def body(r, carry):
        here = pl.ds(pl.multiple_of(r * step, step), step)
        total = None
        for s in range(len(slabs)):
            for k in range(TILE // LANES):
                row = s * (TILE // LANES) + k
                term = slabs[s][here, k * LANES : (k + 1) * LANES] * v_ref[row : row + 1, :]
                total = term if total is None else total + term
        acc_ref[pl.ds(pl.multiple_of(at + r * step, step), step), :] = total
        return carry

    lax.fori_loop(0, slabs[0].shape[0] // step, body, 0)


def cells_kernel(y_ref, ynorm_ref):
    norms(y_ref, ynorm_ref)


def join_kernel(ynorm_ref, got_refs, out_ref, start_ref):
    for d, got_ref in enumerate(got_refs):
        out_ref[d * LANES : (d + 1) * LANES, :] = got_ref[...]
    start_ref[...] = ynorm_ref[0 : start_ref.shape[0], :]


def first_kernel(g, x_ref, y_ref, ynorm_ref, before_ref, m_ref, bound_ref, xnorm_ref, out_ref,
                 v_ref, acc_ref, top_ref, row_ref):
    rows, depth = x_ref.shape
    blocks = rows // LANES
    slabs = len(m_ref)
    scale = 2.0 * LOG2E / (EPS * depth)
    norms(x_ref, xnorm_ref)
    most_x = jnp.max(xnorm_ref[0:blocks, :], keepdims=True)
    most_y = jnp.max(ynorm_ref[...], keepdims=True)
    bound = scale * jnp.sqrt(most_x * most_y)
    bound_ref[...] = jnp.broadcast_to(bound, bound_ref.shape)
    fast = jnp.max(bound) <= LIMIT
    c_bits = ynorm_ref[...] * (-LOG2E / (EPS * depth))
    top_c = jnp.max(c_bits, keepdims=True)

    def scores(s, here=slice(None)):
        ys = y_ref[s * TILE : (s + 1) * TILE, :]
        return lax.dot_general(x_ref[here, :], ys, NT, preferred_element_type=F32) * scale

    @pl.when(fast)
    def _():
        v_ref[...] = jnp.exp2(c_bits - top_c + SHIFT)
        for s in range(slabs):
            power = jnp.exp2(scores(s))
            m_ref[s][...] = power
            total = None if s == 0 else acc_ref[...]
            for k in range(TILE // LANES):
                row = s * (TILE // LANES) + k
                term = power[:, k * LANES : (k + 1) * LANES] * v_ref[row : row + 1, :]
                total = term if total is None else total + term
            acc_ref[...] = total
        top_ref[...] = jnp.broadcast_to(top_c - SHIFT, top_ref.shape)

    @pl.when(jnp.logical_not(fast))
    def _():
        v_ref[...] = c_bits

        def piece(r, carry):
            here = pl.ds(pl.multiple_of(r * 64, 64), 64)
            for s in range(slabs):
                m_ref[s][here, :] = scores(s, here)
            return carry

        lax.fori_loop(0, rows // 64, piece, 0)
        careful_rows(m_ref, v_ref, acc_ref, top_ref, 0)

    row_ref[...] = before_ref[...]
    for d in range(blocks):
        here = slice(d * LANES, (d + 1) * LANES)
        total = log2(lane_sums(acc_ref[here, :])) + top_ref[here, :].T[0:1, :]
        row_ref[pl.ds(holder(g * blocks + d, blocks, before_ref.shape[0] // blocks), 1), :] = total
    out_ref[...] = row_ref[...] if out_ref.ndim == 2 else jnp.broadcast_to(row_ref[...][None], out_ref.shape)


def row_kernel(log_ends, m_ref, bounds, got_ref, out_ref, v_ref, c_ref, acc_ref, top_ref, row_ref):
    slabs = len(m_ref) // len(bounds)
    rows = m_ref[0].shape[0]
    blocks = rows // LANES
    c_ref[...] = log_ends - combine(got_ref[...])
    top_c = jnp.max(c_ref[...], keepdims=True)
    v_ref[...] = jnp.exp2(c_ref[...] - top_c + SHIFT)
    quick = all_fast(bounds)

    def finish(g, at, shift):
        for d in range(blocks):
            here = slice(at + d * LANES, at + (d + 1) * LANES)
            place = pl.ds(holder(g * blocks + d, blocks, len(bounds)), 1)
            row_ref[place, :] = log2(lane_sums(acc_ref[here, :])) + shift(here)

    @pl.when(quick)
    def _():
        for g in range(len(bounds)):
            fast_rows(m_ref[g * slabs : (g + 1) * slabs], v_ref, acc_ref, g * rows)
        for b in range(len(bounds) * blocks):
            row_ref[pl.ds(holder(b, blocks, len(bounds)), 1), :] = lane_sums(acc_ref[b * LANES : (b + 1) * LANES, :])
        row_ref[...] = log2(row_ref[...]) + (top_c - SHIFT)

    for g in range(len(bounds)):
        fast = is_fast(bounds[g])
        part = m_ref[g * slabs : (g + 1) * slabs]

        @pl.when(jnp.logical_not(quick) & fast)
        def _():
            fast_rows(part, v_ref, acc_ref, 0, 16)
            finish(g, 0, lambda here: top_c - SHIFT)

        @pl.when(jnp.logical_not(fast))
        def _():
            careful_rows(part, c_ref, acc_ref, top_ref, 0)
            finish(g, 0, lambda here: top_ref[here, :].T[0:1, :])

    out_ref[...] = jnp.broadcast_to(row_ref[...][None], out_ref.shape)


def col_kernel(log_cells, m_ref, bounds, got_ref, out_ref, u_ref, f_ref, sum_ref):
    slabs = len(m_ref) // len(bounds)
    rows = m_ref[0].shape[0]
    fast = all_fast(bounds)
    f_bits = log_cells - combine(got_ref[...])
    top_f = jnp.max(f_bits, keepdims=True)
    step = 64
    n = slabs * (TILE // LANES)

    def place():
        for b in range(rows * len(bounds) // LANES):
            spread(f_ref[pl.ds(holder(b, rows // LANES, len(bounds)), 1), :], u_ref, b * LANES)

    @pl.when(fast)
    def _():
        f_ref[...] = jnp.exp2(f_bits - top_f + SHIFT)
        place()
        totals = (jnp.zeros((8, LANES), F32),) * n
        for g in range(len(bounds)):

            def body(r, totals):
                here = pl.ds(pl.multiple_of(r * step, step), step)
                u = u_ref[pl.ds(pl.multiple_of(g * rows + r * step, step), step), :]
                new = []
                for s in range(slabs):
                    for k in range(TILE // LANES):
                        term = m_ref[g * slabs + s][here, k * LANES : (k + 1) * LANES] * u
                        total = totals[len(new)]
                        for part in range(step // 8):
                            total = total + term[part * 8 : (part + 1) * 8, :]
                        new.append(total)
                return tuple(new)

            totals = lax.fori_loop(0, rows // step, body, totals)
        for k in range(n):
            sum_ref[k : k + 1, :] = jnp.sum(totals[k], axis=0, keepdims=True)
        sum_ref[...] = log2(sum_ref[...]) + (top_f - SHIFT)

    @pl.when(jnp.logical_not(fast))
    def _():
        f_ref[...] = f_bits
        place()
        step = 8
        for s in range(slabs):

            def score(g, r):
                here = pl.ds(pl.multiple_of(r * step, step), step)
                u = u_ref[pl.ds(pl.multiple_of(g * rows + r * step, step), step), :]
                u = jnp.concatenate([u] * (TILE // LANES), axis=1)
                return score_of(is_fast(bounds[g]), m_ref[g * slabs + s][here, :]) + u

            def add(g, r, carry):
                top, total = carry
                new = score(g, r)
                most = jnp.maximum(top, new)
                return most, total * jnp.exp2(top - most) + jnp.exp2(new - most)

            carry = jnp.full((step, TILE), -3.0e38, F32), jnp.zeros((step, TILE), F32)
            for g in range(len(bounds)):
                carry = lax.fori_loop(0, rows // step, functools.partial(add, g), carry)
            tops, total = carry
            top = jnp.max(tops, axis=0, keepdims=True)
            total = jnp.sum(total * jnp.exp2(tops - top), axis=0, keepdims=True)
            total = log2(total) + top
            for k in range(TILE // LANES):
                row = s * (TILE // LANES) + k
                sum_ref[row : row + 1, :] = total[:, k * LANES : (k + 1) * LANES]

    out_ref[...] = jnp.broadcast_to(sum_ref[...][None], out_ref.shape)


def last_kernel(g, log_cells, log_ends, m_ref, bounds, xnorms, rows_ref, cols_ref, y_ref, ynorm_ref, before_ref,
                out_ref, after_ref, *rest):
    *pots, f_ref, u_ref, v_ref, mass_ref, row_ref = rest
    slabs = len(m_ref)
    rows, depth = m_ref[0].shape[0], y_ref.shape[1]
    blocks = rows // LANES
    fast = is_fast(bounds[g])
    f_bits = log_cells - combine(rows_ref[...])
    c_bits = log_ends - combine(cols_ref[...])
    f_ref[...] = f_bits
    mine = [f_ref[pl.ds(holder(g * blocks + d, blocks, len(bounds)), 1), :] for d in range(blocks)]
    top_f = jnp.max(functools.reduce(jnp.maximum, mine), keepdims=True) - 24.0

    def weigh(here, weight):
        u = u_ref[here, :]
        moved = None
        mass = None
        for s in range(slabs):
            parts = []
            for k in range(TILE // LANES):
                row = s * (TILE // LANES) + k
                part = weight(m_ref[s][here, k * LANES : (k + 1) * LANES], u, v_ref[row : row + 1, :])
                mass = part if mass is None else mass + part
                parts.append(part.astype(BF16))
            term = jnp.dot(jnp.concatenate(parts, axis=1), y_ref[s * TILE : (s + 1) * TILE, :], preferred_element_type=F32)
            moved = term if moved is None else moved + term
        mass_ref[here, :] = mass
        out_ref[here, :] = moved.astype(out_ref.dtype)

    @pl.when(fast)
    def _():
        v_ref[...] = jnp.exp2(c_bits + (top_f - log_cells))
        for d in range(blocks):
            spread(jnp.exp2(mine[d] - top_f), u_ref, d * LANES)
        weigh(slice(0, rows), lambda m, u, v: (m * u) * v)

    @pl.when(jnp.logical_not(fast))
    def _():
        v_ref[...] = c_bits - log_cells
        for d in range(blocks):
            spread(mine[d], u_ref, d * LANES)
        step = 16

        def body(r, carry):
            here = pl.ds(pl.multiple_of(r * step, step), step)
            weigh(here, lambda m, u, v: jnp.exp2((m + u) + v))
            return carry

        lax.fori_loop(0, rows // step, body, 0)

    row_ref[...] = jnp.zeros_like(row_ref)
    for d in range(blocks):
        row_ref[d : d + 1, :] = lane_sums(mass_ref[d * LANES : (d + 1) * LANES, :])
    mass = row_ref[...]
    if out_ref.dtype == F32:
        out_ref[rows : rows + 8, :] = jnp.concatenate([mass, mass], axis=1)
    else:
        high = mass.astype(BF16).astype(F32)
        mid = (mass - high).astype(BF16).astype(F32)
        low = mass - high - mid
        first = jnp.concatenate([high, mid], axis=1)
        second = jnp.concatenate([low, low], axis=1)
        out_ref[rows : rows + 16, :] = jnp.concatenate([first, second], axis=0).astype(BF16)
    after_ref[...] = before_ref[...]
    if pots:
        end_ref, cell_ref = pots
        for p, xnorm_ref in enumerate(xnorms):
            for d in range(blocks):
                f_ref[pl.ds(holder(p * blocks + d, blocks, len(bounds)), 1), :] = xnorm_ref[d : d + 1, :]
        end_ref[...] = f_bits * (EPS / LOG2E) + f_ref[...] * (1.0 / depth)
        cell_ref[...] = c_bits * (EPS / LOG2E) + ynorm_ref[...] * (1.0 / depth)


def sum_kernel(own_ref, got_refs, out_refs):
    rows = own_ref.shape[0] - 8
    mass = own_ref[rows : rows + 8, :LANES]
    for got_ref in got_refs:
        parts = got_ref[rows : rows + 16, :].astype(F32)
        mass = mass + ((parts[0:8, :LANES] + parts[0:8, LANES:]) + parts[8:16, :LANES])
    wide = jnp.concatenate([mass, mass], axis=1)
    for d, out_ref in enumerate(out_refs):
        here = slice(d * LANES, (d + 1) * LANES)
        total = own_ref[here, :]
        for got_ref in got_refs:
            total = total + got_ref[here, :].astype(F32)
        out_ref[0:LANES, :] = total
        out_ref[LANES : LANES + 8, :] = jnp.broadcast_to(wide[d : d + 1, :], (8, wide.shape[1]))


def end_kernel(x_ref, got_refs, out_ref):
    total = functools.reduce(jnp.add, [got_ref[...] for got_ref in got_refs])
    wide = jnp.broadcast_to(total[LANES : LANES + 1, :LANES], (LANES, LANES)).T
    x = x_ref[...].astype(F32)
    out_ref[:, :LANES] = x[:, :LANES] * wide - total[:LANES, :LANES]
    out_ref[:, LANES:] = x[:, LANES:] * wide - total[:LANES, LANES:]


def grouped(kernel, at, *counts):
    def body(*refs):
        groups, n = [], at
        for count in counts:
            groups.append(refs[n : n + count] if count else refs[n])
            n += max(count, 1)
        kernel(*refs[:at], *groups, *refs[n:])

    body.__name__ = getattr(kernel, "func", kernel).__name__
    return body


def call(kernel, outs, scratch, limit_mib=16, cost=None):
    return pl.pallas_call(
        kernel,
        name=getattr(kernel, "func", kernel).__name__,
        out_shape=outs,
        cost_estimate=cost,
        scratch_shapes=[pltpu.VMEM(s, F32) for s in scratch],
        compiler_params=pltpu.CompilerParams(vmem_limit_bytes=limit_mib << 20),
    )


def swap(parts, axis):
    return lax.all_to_all(parts, axis, 0, 0, tiled=True)


def flip(value, by, turned):
    n_row, n_col = lax.axis_size("row"), lax.axis_size("col")
    pairs = [(r * n_col + n, r * n_col + (n ^ (turned if r % 2 else by))) for r in range(n_row) for n in range(n_col)]
    return lax.ppermute(value, ("row", "col"), pairs)


def pin(m):
    return pltpu.with_memory_space_constraint(m, pltpu.VMEM)


def inside(*shape, dtype=F32):
    return pltpu.VMEM(shape, dtype)


def shards(endpoints, cells):
    n_row, n_col = lax.axis_size("row"), lax.axis_size("col")
    nx = 1 << ((n_col.bit_length() - 1) // 2)
    ny = n_col // nx
    square = nx == ny

    def between(value, d):
        return flip(value, d, d * ny if square else d)

    def across(value, g):
        return flip(value, g * nx, g if square else g * nx)

    own, depth = endpoints.shape
    rows, cols, part = own * n_col, cells.shape[0], own * nx
    log_cells = math.log2(cols * n_col)
    log_ends = math.log2(rows * n_row)
    rb, cb, slabs = rows // LANES, cols // LANES, cols // TILE
    order = sorted(range(1, ny), key=lambda g: min(g, ny - g))
    work = 2 * part * cols * depth
    small = pl.CostEstimate(flops=work // 16, bytes_accessed=part * cols // 4, transcendentals=0)
    cost = pl.CostEstimate(flops=work, bytes_accessed=4 * part * cols, transcendentals=0)

    ynorm = call(cells_kernel, inside(cb, LANES), [], cost=cost)(pin(cells))
    near, sums = call(
        grouped(join_kernel, 1, nx),
        [inside(part, depth, dtype=BF16), inside(rb, LANES)],
        [],
    )(pin(ynorm), *[pin(between(endpoints, d)) if d else endpoints for d in range(nx)])
    x = [near] + [across(near, g) for g in range(1, ny)]

    m, bounds, xnorms = [None] * ny, [None] * ny, [None] * ny
    for g in [0] + order:
        out = inside(n_col, rb, LANES) if g == order[-1] else inside(rb, LANES)
        *m[g], bounds[g], xnorms[g], sums = call(
            grouped(functools.partial(first_kernel, g), 4, slabs),
            [inside(part, TILE)] * slabs + [inside(8, LANES), inside(8, LANES), out],
            [(cb, LANES), (part, LANES), (part, LANES), (rb, LANES)],
            cost=cost,
        )(pin(x[g]), pin(cells), pin(ynorm), pin(sums))
    block = [pin(slab) for g in range(ny) for slab in m[g]]
    flags = [pin(bound) for bound in bounds]

    for step in range(ITERS):
        if step > 0:
            sums = call(
                grouped(functools.partial(row_kernel, log_ends), 0, ny * slabs, ny),
                inside(n_col, rb, LANES),
                [(cb, LANES), (cb, LANES), (rows, LANES), (part, LANES), (rb, LANES)],
            )(*block, *flags, pin(got_cols))
        got_rows = swap(sums, "col")
        sums = call(
            grouped(functools.partial(col_kernel, log_cells), 0, ny * slabs, ny),
            inside(n_row, cb, LANES),
            [(rows, LANES), (rb, LANES), (cb, LANES)],
        )(*block, *flags, pin(got_rows))
        got_cols = swap(sums, "row")

    token = inside(8, LANES)
    sent, after = [], bounds[0]
    for g in order[::-1] + [0]:
        message = inside(part + 16, depth, dtype=BF16) if g else inside(part + 8, depth)
        pots = [] if g else [jax.ShapeDtypeStruct((rb, LANES), F32), jax.ShapeDtypeStruct((cb, LANES), F32)]
        message, after, *pots = call(
            grouped(functools.partial(last_kernel, g, log_cells, log_ends), 0, slabs, ny, ny),
            [message, token] + pots,
            [(rb, LANES), (part, LANES), (cb, LANES), (part, LANES), (8, LANES)],
            cost=small,
        )(*map(pin, m[g]), *flags, *map(pin, xnorms), pin(got_rows), pin(got_cols), pin(cells), pin(ynorm), pin(after))
        sent.append(across(message, g) if g else message)
    end_pot, cell_pot = pots
    sums = call(
        grouped(sum_kernel, 0, 0, ny - 1, nx),
        [inside(own + 8, depth)] * nx,
        [],
    )(pin(sent[-1]), *map(pin, sent[:-1]))
    sums = [sums[0]] + [between(sums[d], d) for d in range(1, nx)]
    displacement = call(
        grouped(end_kernel, 1, nx),
        jax.ShapeDtypeStruct((own, depth), F32),
        [],
    )(endpoints, *map(pin, sums))
    return end_pot.reshape(rows), cell_pot.reshape(cols), displacement


def solution(mesh):
    return jax.shard_map(
        shards,
        mesh=mesh,
        in_specs=(P(("row", "col"), None), P("col", None)),
        out_specs=(P("row"), P("col"), P(("row", "col"), None)),
        check_vma=False,
    )
```
